256 devices in a mesh: dp: 32 (over x, z_lo, y), tensor: 8 (over z_hi, core).
Axes of the slice: x: 4, y: 4, z: 8 (z_hi: 4, z_lo: 2; z = z_hi * 2 + z_lo), core: 2. Of those that a mesh axis runs over, the one named last changes fastest.
Arguments:
- activations: bfloat16 [32768, 28672], P('dp', 'tensor'), may hold values from -6 to 6
- out_grads: bfloat16 [32768, 8192], P('dp', 'tensor'), may hold values from -6 to 6
- proj_in: bfloat16 [28672, 64], P('tensor'), may hold values from -0.03125 to 0.03125
- proj_out: bfloat16 [8192, 64], P('tensor'), may hold values from -0.0625 to 0.0625
- doc_ids: int32 [32, 1024], P('dp'), may hold values from 0 to 3, never falling along the last dimension, each value on 1 to 512 neighbouring positions
- queries: bfloat16 [8192, 4096], P(('dp', 'tensor')), may hold values from -0.005859375 to 0.005859375
- block_owner: int32 [32], replicated, may hold values from 0 to 31, each once
Outputs:
- scores: float32 [8192, 128], P(('dp', 'tensor'))
The draws below stay inside these ranges and needn't reach their ends.
Inputs may be any that keep to these rules, and one draw needn't show every extreme that they name: `doc_ids`: each index of dp holds 4 documents as runs of consecutive tokens in rising order, each of 1 to 512 tokens, one of exactly that many. `block_owner`: a permutation.
All inputs are finite; a program needn't handle non-finite values.
Results may differ from the reference program's by a relative error of at most 0.0029.
Values may be sent and summed in bfloat16 or wider, within the bound.
No kernel may reach another device: no remote copies, remote signals or barrier semaphores. Data moves between devices by JAX's collectives and lax.ppermute only.
A program may use at most 64 MiB of HBM per device.

```python
import math
import jax
import jax.numpy as jnp
import numpy as np
from jax import lax

D = 8192
FF = 28672
RANK = 64
TOK_DEV = 1024
DOCS_DEV = 4
FEAT = 4096
TOKENS = 32768
NQ = 8192
N_DP = 32


def levels(key, dims, shards, least, top_value):
    def one(position, shards_of):
        heights = jax.random.uniform(jax.random.fold_in(jax.random.fold_in(key, 6), position), (shards_of,), jnp.float32, least / len(shards), top_value / len(shards))
        return jnp.repeat(jnp.exp(heights), dims[position] // shards_of).reshape((-1,) + (1,) * (len(dims) - position - 1))

    level = one(*shards[0])
    for cut in shards[1:]:
        level = level * one(*cut)
    return level


def split_up(amount, total, most, skew):
    weights = [(1 << 20) // math.isqrt(grade ** skew) + 1 for grade in range(2, amount + 1)]
    spare, given = total - most - (amount - 1), [1] * (amount - 1)
    while spare > 0:
        free = [i for i in range(amount - 1) if given[i] < most]
        mass, budget = sum([weights[i] for i in free]), spare
        for i in free:
            addition = min(most - given[i], max(1, budget * weights[i] // mass), spare)
            given[i] = given[i] + addition
            spare = spare - addition
    return np.array([most] + given)


def uneven(key, amount, total, most, slope):
    if amount == 2:
        one = jax.random.randint(key, (), max(1, total - most), min(most, total - 1) + 1)
        return jnp.stack([one, total - one])
    sizes = jnp.asarray(split_up(amount, total, most, slope), jnp.int32)
    couples = (amount - 1) // 2
    source_of, receiver = sizes[1:1 + 2 * couples:2], sizes[2:2 + 2 * couples:2]
    room = jnp.minimum(source_of - 1, most - receiver)
    shifted = jax.random.randint(jax.random.fold_in(key, 1), (couples,), 0, 1 << 20) % (room + 1)
    sizes = sizes.at[1:1 + 2 * couples:2].set(source_of - shifted).at[2:2 + 2 * couples:2].set(receiver + shifted)
    return sizes[jax.random.permutation(jax.random.fold_in(key, 2), amount)]


def gaussian(own_key, extent, width, most, pieces=(), kind=jnp.bfloat16):
    result = jax.random.normal(own_key, extent, jnp.float32) * width
    if len(pieces) > 0:
        result = levels(own_key, extent, pieces, -0.22, 0.18) * result
    return jnp.clip(result, min=-most, max=most).astype(kind)


def setup_inputs(seed: int = 0) -> dict:
    arg_keys = jax.random.split(jax.random.key(seed), 8)
    activations = gaussian(arg_keys[0], (TOKENS, FF), 1.0, 6.0, ((0, 32), (1, 8)))
    out_grads = gaussian(arg_keys[1], (TOKENS, D), 1.0, 6.0, ((0, 32), (1, 8)))
    proj_in = gaussian(arg_keys[2], (FF, RANK), FF ** -0.5, 0.03125, ((0, 8),))
    proj_out = gaussian(arg_keys[3], (D, RANK), D ** -0.5, 0.0625, ((0, 8),))
    doc_ids = jax.vmap(lambda own: jnp.searchsorted(jnp.cumsum(uneven(own, DOCS_DEV, TOK_DEV, TOK_DEV // 2, 2)), jnp.arange(TOK_DEV), side="right"))(jax.random.split(arg_keys[4], N_DP)).reshape((N_DP, TOK_DEV)).astype(jnp.int32)
    queries = gaussian(arg_keys[5], (NQ, FEAT), (FEAT * TOK_DEV // DOCS_DEV) ** -0.5, 0.005859375, ((0, 256),))
    block_owner = jax.random.permutation(arg_keys[6], N_DP).astype(jnp.int32)
    return dict(activations=activations, out_grads=out_grads, proj_in=proj_in, proj_out=proj_out, doc_ids=doc_ids, queries=queries, block_owner=block_owner)


def reference(activations, out_grads, proj_in, proj_out, doc_ids, queries, block_owner):
    in_proj = jnp.dot(activations, proj_in, preferred_element_type=jnp.float32)
    out_proj = jnp.dot(out_grads, proj_out, preferred_element_type=jnp.float32)
    in_proj = in_proj.reshape(N_DP, TOK_DEV, RANK)
    out_proj = out_proj.reshape(N_DP, TOK_DEV, RANK)
    labels = jnp.arange(DOCS_DEV, dtype=jnp.int32)
    onehot = (doc_ids[:, None, :] == labels[None, :, None]).astype(jnp.float32)
    weighted = onehot[:, :, :, None] * out_proj[:, None, :, :]
    features = jnp.einsum("pdti,ptj->pdij", weighted, in_proj, precision=lax.Precision.HIGHEST)
    doc_feat = features.reshape(N_DP * DOCS_DEV, RANK * RANK).astype(jnp.bfloat16)
    stored = jnp.dot(queries, doc_feat.T, preferred_element_type=jnp.float32)
    blocks = stored.reshape(N_DP, stored.shape[0] // N_DP, stored.shape[1])
    return blocks[block_owner].reshape(stored.shape)
```

```python
import jax
import jax.numpy as jnp
from jax import lax
from jax.sharding import PartitionSpec as P

RANK = 64
DOCS_DEV = 4
N_DP = 32
HALF = RANK // 2


def swap(value, bits):
    return lax.ppermute(value, "tensor", [(i, i ^ bits) for i in range(8)])


def pick(first, low, high):
    return jnp.where(first, low, high), jnp.where(first, high, low)


def shards(activations, out_grads, proj_in, proj_out, doc_ids, queries, block_owner):
    me = lax.axis_index("tensor")
    core0, chip = (me & 1) == 0, me >> 1
    row0, col0 = (chip >> 1) == 0, (chip & 1) == 0

    cut = queries.reshape(32, 2, 2, 16, 2, HALF)
    mine, other = pick(core0, cut[:, :, 0], cut[:, :, 1])
    got = swap(other, 1)
    rows0 = jnp.where(core0, mine, got)
    rows1 = jnp.where(core0, got, mine)
    q = jnp.stack([rows0, rows1]).reshape(64, 2, 16, 2, HALF).transpose(0, 1, 3, 2, 4).reshape(64, 2048)

    part_out = jnp.dot(out_grads, proj_out, preferred_element_type=jnp.float32).T
    part_in = jnp.dot(activations, proj_in, preferred_element_type=jnp.float32).T
    part = jnp.concatenate([part_out.reshape(2, HALF, -1), part_in.reshape(2, HALF, -1)])
    half = part.shape[-1] // 2
    keep, send = pick(core0, part[..., :half], part[..., half:])
    total = keep + swap(send, 1)
    out_keep, out_other = pick(row0, total[0], total[1])
    in_keep, in_other = pick(col0, total[2], total[3])
    far = swap(jnp.stack([out_other, in_keep]), 4)
    near = swap(jnp.stack([out_keep, in_other]), 2)
    last = swap(jnp.stack([out_other, in_other]), 6)
    out_proj, in_proj = (jnp.stack([out_keep, in_keep]) + near) + (far + last)

    ids = doc_ids[0]
    labels_now = jnp.where(core0, ids[:half], ids[half:])
    labels = jnp.arange(DOCS_DEV, dtype=jnp.int32)
    onehot = (labels_now[None, :] == labels[:, None]).astype(jnp.float32)
    weighted = onehot[:, None, :] * out_proj[None]
    feat = jnp.einsum("dit,jt->dij", weighted, in_proj, precision=lax.Precision.HIGHEST)
    keep, send = pick(core0, feat[:, :16], feat[:, 16:])
    block = (keep + swap(send, 1)).astype(jnp.bfloat16).reshape(DOCS_DEV, 512)

    groups = [[p * 8 + 2 * b + c for p in range(N_DP) for b in range(4)] for c in range(2)]
    everyone = jnp.broadcast_to(block, (4 * N_DP, DOCS_DEV, 512))
    feats = lax.all_to_all(everyone, ("dp", "tensor"), 0, 0, axis_index_groups=groups)
    feats = feats.reshape(N_DP, 4, DOCS_DEV, 512).transpose(0, 2, 1, 3).reshape(N_DP * DOCS_DEV, 2048)
    scored = lax.dot_general(q, feats, (((1,), (1,)), ((), ())), preferred_element_type=jnp.float32)
    keep, send = pick(core0, scored[:32], scored[32:])
    stored = (keep + swap(send, 1)).astype(jnp.bfloat16)

    blocks = lax.all_to_all(jnp.broadcast_to(stored, (N_DP,) + stored.shape), "dp", 0, 0)
    owner = block_owner[lax.axis_index("dp")]
    return lax.dynamic_index_in_dim(blocks, owner, 0, keepdims=False).astype(jnp.float32)


def solution(mesh):
    placed = (
        P("dp", "tensor"),
        P("dp", "tensor"),
        P("tensor", None),
        P("tensor", None),
        P("dp", None),
        P(("dp", "tensor"), None),
        P(),
    )
    return jax.shard_map(
        shards, mesh=mesh, in_specs=placed, out_specs=P(("dp", "tensor"), None), check_vma=False
    )
```

```python
import jax
import jax.numpy as jnp
from jax import lax
from jax.sharding import PartitionSpec as P

RANK = 64
DOCS_DEV = 4
N_DP = 32
HALF = RANK // 2


def swap(value, bits):
    return lax.ppermute(value, "tensor", [(i, i ^ bits) for i in range(8)])


def pick(first, low, high):
    return jnp.where(first, low, high), jnp.where(first, high, low)


def shards(activations, out_grads, proj_in, proj_out, doc_ids, queries, block_owner):
    me = lax.axis_index("tensor")
    core0, chip = (me & 1) == 0, me >> 1
    row0, col0 = (chip >> 1) == 0, (chip & 1) == 0

    part_out = jnp.dot(out_grads, proj_out, preferred_element_type=jnp.float32).T
    part_in = jnp.dot(activations, proj_in, preferred_element_type=jnp.float32).T
    part = jnp.concatenate([part_out.reshape(2, HALF, -1), part_in.reshape(2, HALF, -1)])
    half = part.shape[-1] // 2
    keep, send = pick(core0, part[..., :half], part[..., half:])
    total = keep + swap(send, 1)
    queries, total = lax.optimization_barrier((queries, total))
    cut = queries.reshape(32, 2, 2, 16, 2, HALF).transpose(1, 4, 2, 0, 3, 5).reshape(8, 32, 512)
    out_keep, out_other = pick(row0, total[0], total[1])
    in_keep, in_other = pick(col0, total[2], total[3])
    far = swap(jnp.stack([out_other, in_keep]), 4)
    near = swap(jnp.stack([out_keep, in_other]), 2)
    last = swap(jnp.stack([out_other, in_other]), 6)
    near, far, last, cut = lax.optimization_barrier((near, far, last, cut))
    out_proj, in_proj = (jnp.stack([out_keep, in_keep]) + near) + (far + last)

    ids = doc_ids[0]
    labels_now = jnp.where(core0, ids[:half], ids[half:])
    labels = jnp.arange(DOCS_DEV, dtype=jnp.int32)
    onehot = (labels_now[None, :] == labels[:, None]).astype(jnp.float32)
    weighted = onehot[:, None, :] * out_proj[None]
    feat = jnp.einsum("dit,jt->dij", weighted, in_proj, precision=lax.Precision.HIGHEST)
    keep, send = pick(core0, feat[:, :16], feat[:, 16:])
    block = (keep + swap(send, 1)).astype(jnp.bfloat16).reshape(DOCS_DEV, 512)

    block, cut = lax.optimization_barrier((block, cut))
    feats = lax.all_to_all(jnp.broadcast_to(block, (N_DP, DOCS_DEV, 512)), "dp", 0, 0)
    feats = feats.reshape(N_DP * DOCS_DEV, 512)
    q = lax.all_to_all(cut, "tensor", 0, 0).reshape(256, 512)
    scored = lax.dot_general(q, feats, (((1,), (1,)), ((), ())), preferred_element_type=jnp.float32)
    parts = lax.all_to_all(scored.reshape(8, 32, N_DP * DOCS_DEV), "tensor", 0, 0)
    stored = jnp.sum(parts, axis=0).astype(jnp.bfloat16)

    blocks = lax.all_to_all(jnp.broadcast_to(stored, (N_DP,) + stored.shape), "dp", 0, 0)
    owner = block_owner[lax.axis_index("dp")]
    return lax.dynamic_index_in_dim(blocks, owner, 0, keepdims=False).astype(jnp.float32)


def solution(mesh):
    placed = (
        P("dp", "tensor"),
        P("dp", "tensor"),
        P("tensor", None),
        P("tensor", None),
        P("dp", None),
        P(("dp", "tensor"), None),
        P(),
    )
    return jax.shard_map(
        shards, mesh=mesh, in_specs=placed, out_specs=P(("dp", "tensor"), None), check_vma=False
    )
```

```python
import jax
import jax.numpy as jnp
from jax import lax
from jax.experimental import pallas as pl
from jax.experimental.pallas import tpu as pltpu
from jax.sharding import PartitionSpec as P

RANK = 64
DOCS_DEV = 4
N_DP = 32
DOCS = N_DP * DOCS_DEV
TOKENS = 1024
STEP = 256
NT = (((1,), (1,)), ((), ()))


def swap(value, bits):
    return lax.ppermute(value, "tensor", [(i, i ^ bits) for i in range(8)])


def pick(first, low, high):
    return jnp.where(first, low, high), jnp.where(first, high, low)


def project_kernel(out_grads, activations, proj_out, proj_in, part):
    from_out = lax.dot_general(out_grads[...], proj_out[...], NT, preferred_element_type=jnp.float32)
    from_in = lax.dot_general(activations[...], proj_in[...], NT, preferred_element_type=jnp.float32)
    part[...] = jnp.concatenate([from_out, from_in], axis=1)


def project(out_grads, activations, proj_out, proj_in):
    d, ff = out_grads.shape[1], activations.shape[1]
    return pl.pallas_call(
        project_kernel,
        grid=(TOKENS // STEP,),
        in_specs=[
            pl.BlockSpec((STEP, d), lambda i: (i, 0)),
            pl.BlockSpec((STEP, ff), lambda i: (i, 0)),
            pl.BlockSpec((RANK, d), lambda i: (0, 0)),
            pl.BlockSpec((RANK, ff), lambda i: (0, 0)),
        ],
        out_specs=pl.BlockSpec((STEP, 2 * RANK), lambda i: (i, 0)),
        out_shape=jax.ShapeDtypeStruct((TOKENS, 2 * RANK), jnp.float32),
        compiler_params=pltpu.CompilerParams(vmem_limit_bytes=60 << 20),
        name="project",
    )(out_grads, activations, proj_out, proj_in)


def features_kernel(ids, p, p_more, q, q_more, feat):
    both = jnp.concatenate([p[...] + p_more[...], q[...] + q_more[...]], axis=0)
    out_t = both.T[:RANK]
    weighted = jnp.concatenate([jnp.where(ids[...] == d, out_t, 0.0) for d in range(DOCS_DEV)], axis=0)
    feat[...] = jnp.dot(
        weighted, both[:, RANK:], precision=lax.Precision.HIGHEST, preferred_element_type=jnp.float32
    )


def features(ids, p, p_more, q, q_more):
    return pl.pallas_call(
        features_kernel,
        out_shape=jax.ShapeDtypeStruct((DOCS_DEV * RANK, RANK), jnp.float32),
        compiler_params=pltpu.CompilerParams(vmem_limit_bytes=16 << 20),
        name="features",
    )(ids, p, p_more, q, q_more)


def score_kernel(mine, got, feats, scored):
    half = feats.shape[1]
    rows = jnp.concatenate([mine[:, :half], got[:, :half], mine[:, half:], got[:, half:]], axis=0)
    every = lax.dot_general(rows, feats[...], NT, preferred_element_type=jnp.float32)
    source = lax.broadcasted_iota(jnp.int32, (2 * DOCS, DOCS), 0)
    doc = lax.broadcasted_iota(jnp.int32, (2 * DOCS, DOCS), 1)
    first = (doc >> 2) * 8 + (doc & 3)
    count = rows.shape[0] // 2
    scored[...] = jnp.dot(
        every[:count], (source == first).astype(jnp.float32), precision=lax.Precision.HIGHEST,
        preferred_element_type=jnp.float32,
    ) + jnp.dot(
        every[count:], (source == first + 4).astype(jnp.float32), precision=lax.Precision.HIGHEST,
        preferred_element_type=jnp.float32,
    )


def score(mine, got, feats):
    return pl.pallas_call(
        score_kernel,
        out_shape=jax.ShapeDtypeStruct((2 * mine.shape[0], DOCS), jnp.float32),
        compiler_params=pltpu.CompilerParams(vmem_limit_bytes=16 << 20),
        name="score",
    )(mine, got, feats)


def shards(activations, out_grads, proj_in, proj_out, doc_ids, queries, block_owner):
    core0 = (lax.axis_index("tensor") & 1) == 0
    half = TOKENS // 2

    part = project(out_grads, activations, proj_out.T, proj_in.T)
    keep, send = pick(core0, part[:half], part[half:])
    total = keep + swap(send, 1)
    p, q = total[: half // 2], total[half // 2 :]
    p, q = p + swap(p, 6), q + swap(q, 2)
    p_more, q_more = swap(p, 2), swap(q, 6)

    columns = queries.shape[1] // 2
    mine, other = pick(core0, queries[:, :columns], queries[:, columns:])
    got = swap(other, 1)

    ids = jnp.where(core0, doc_ids[:, :half], doc_ids[:, half:])
    feat = features(ids, p, p_more, q, q_more).reshape(DOCS_DEV, 2, RANK // 2, RANK)
    keep, send = pick(core0, feat[:, 0], feat[:, 1])
    block = (keep + swap(send, 1)).astype(jnp.bfloat16)
    block = block.reshape(DOCS_DEV, 2, columns // 2).transpose(1, 0, 2).reshape(2 * DOCS_DEV, columns // 2)

    everyone = jnp.broadcast_to(block, (N_DP,) + block.shape)
    feats = lax.all_to_all(everyone, "dp", 0, 0).reshape(2 * DOCS, columns // 2)
    scored = score(mine, got, feats)
    rows = queries.shape[0]
    stored = (scored[:rows] + swap(scored[rows:], 1)).astype(jnp.bfloat16)

    blocks = lax.all_to_all(jnp.broadcast_to(stored, (N_DP,) + stored.shape), "dp", 0, 0)
    owner = block_owner[lax.axis_index("dp")]
    return lax.dynamic_index_in_dim(blocks, owner, 0, keepdims=False).astype(jnp.float32)


def solution(mesh):
    placed = (
        P("dp", "tensor"),
        P("dp", "tensor"),
        P("tensor", None),
        P("tensor", None),
        P("dp", None),
        P(("dp", "tensor"), None),
        P(),
    )
    return jax.shard_map(
        shards, mesh=mesh, in_specs=placed, out_specs=P(("dp", "tensor"), None), check_vma=False
    )
```

```python
import jax
import jax.numpy as jnp
from jax import lax
from jax.experimental import pallas as pl
from jax.experimental.pallas import tpu as pltpu
from jax.sharding import PartitionSpec as P

RANK = 64
DOCS_DEV = 4
N_DP = 32
DOCS = N_DP * DOCS_DEV
TOKENS = 1024
STEP = 256
NT = (((1,), (1,)), ((), ()))


def swap(value, even, odd):
    return lax.ppermute(value, "tensor", [(i, i ^ (odd if i & 1 else even)) for i in range(8)])


def pick(first, low, high):
    return jnp.where(first, low, high), jnp.where(first, high, low)


def project_kernel(out_grads, activations, proj_out, proj_in, send, keep, grads, acts, raw_out, raw_in, wide_out, wide_in, sem):
    blocks = TOKENS // STEP
    first = jnp.where((lax.axis_index("tensor") & 1) == 0, TOKENS // 2, 0)

    def rows(block):
        start = first + block * STEP
        return pl.ds(pl.multiple_of(jnp.where(start >= TOKENS, start - TOKENS, start), STEP), STEP)

    def copies(block):
        here = pl.ds(pl.multiple_of(block * STEP, STEP), STEP)
        return (
            pltpu.make_async_copy(out_grads.at[rows(block)], grads.at[here], sem.at[2 + 2 * block]),
            pltpu.make_async_copy(activations.at[rows(block)], acts.at[here], sem.at[3 + 2 * block]),
        )

    weights = (
        pltpu.make_async_copy(proj_out, raw_out, sem.at[0]),
        pltpu.make_async_copy(proj_in, raw_in, sem.at[1]),
    )
    for copy in weights:
        copy.start()
    for block in range(blocks):
        for copy in copies(block):
            copy.start()
    for copy in weights:
        copy.wait()
    wide_out[...] = jnp.concatenate([raw_out[...], jnp.zeros_like(raw_out)], axis=0).T
    wide_in[...] = jnp.concatenate([jnp.zeros_like(raw_in), raw_in[...]], axis=0).T

    def run(block, target):
        here = pl.ds(pl.multiple_of(block * STEP, STEP), STEP)
        there = pl.ds(pl.multiple_of(block % (blocks // 2) * STEP, STEP), STEP)
        for copy in copies(block):
            copy.wait()
        target[there] = jnp.dot(grads[here], wide_out[...], preferred_element_type=jnp.float32) + jnp.dot(
            acts[here], wide_in[...], preferred_element_type=jnp.float32
        )

    @pl.loop(0, blocks // 2)
    def _(block):
        run(block, send)

    @pl.loop(blocks // 2, blocks)
    def _(block):
        run(block, keep)


def project(out_grads, activations, proj_out, proj_in):
    d, ff = out_grads.shape[1], activations.shape[1]
    half = pltpu.VMEM((TOKENS // 2, 2 * RANK), jnp.float32)
    args = [pltpu.with_memory_space_constraint(x, pltpu.HBM) for x in (out_grads, activations, proj_out, proj_in)]
    return pl.pallas_call(
        project_kernel,
        in_specs=[pl.BlockSpec(memory_space=pltpu.HBM)] * 4,
        out_specs=[pl.BlockSpec(memory_space=pltpu.VMEM)] * 2,
        out_shape=[half, half],
        scratch_shapes=[
            pltpu.VMEM((TOKENS, d), jnp.bfloat16),
            pltpu.VMEM((TOKENS, ff), jnp.bfloat16),
            pltpu.VMEM((RANK, d), jnp.bfloat16),
            pltpu.VMEM((RANK, ff), jnp.bfloat16),
            pltpu.VMEM((d, 2 * RANK), jnp.bfloat16),
            pltpu.VMEM((ff, 2 * RANK), jnp.bfloat16),
            pltpu.SemaphoreType.DMA((2 + 2 * (TOKENS // STEP),)),
        ],
        compiler_params=pltpu.CompilerParams(vmem_limit_bytes=40 << 20),
        name="project",
    )(*args)


def features_kernel(ids, total, more, feat):
    both = total[...] + more[...]
    out_t = both.T[:RANK]
    weighted = jnp.concatenate([jnp.where(ids[...] == d, out_t, 0.0) for d in range(DOCS_DEV)], axis=0)
    feat[...] = jnp.dot(
        weighted, both[:, RANK:], precision=lax.Precision.HIGHEST, preferred_element_type=jnp.float32
    )


def features(ids, total, more):
    return pl.pallas_call(
        features_kernel,
        out_shape=jax.ShapeDtypeStruct((DOCS_DEV * RANK, RANK), jnp.float32),
        compiler_params=pltpu.CompilerParams(vmem_limit_bytes=16 << 20),
        name="features",
    )(ids, total, more)


def score_kernel(mine, got, feats, scored):
    half = feats.shape[1]
    rows = jnp.concatenate([mine[:, :half], got[:, :half], mine[:, half:], got[:, half:]], axis=0)
    every = lax.dot_general(rows, feats[...], NT, preferred_element_type=jnp.float32)
    source = lax.broadcasted_iota(jnp.int32, (2 * DOCS, DOCS), 0)
    doc = lax.broadcasted_iota(jnp.int32, (2 * DOCS, DOCS), 1)
    first = (doc >> 2) * 8 + (doc & 3)
    count = rows.shape[0] // 2
    scored[...] = jnp.dot(
        every[:count], (source == first).astype(jnp.float32), precision=lax.Precision.HIGHEST,
        preferred_element_type=jnp.float32,
    ) + jnp.dot(
        every[count:], (source == first + 4).astype(jnp.float32), precision=lax.Precision.HIGHEST,
        preferred_element_type=jnp.float32,
    )


def score(mine, got, feats):
    return pl.pallas_call(
        score_kernel,
        out_shape=jax.ShapeDtypeStruct((2 * mine.shape[0], DOCS), jnp.float32),
        compiler_params=pltpu.CompilerParams(vmem_limit_bytes=16 << 20),
        name="score",
    )(mine, got, feats)


def spread_kernel(block, everyone):
    everyone[...] = jnp.broadcast_to(block[...], everyone.shape)


def spread(block):
    return pl.pallas_call(
        spread_kernel,
        out_specs=pl.BlockSpec(memory_space=pltpu.VMEM),
        out_shape=pltpu.VMEM((N_DP,) + block.shape, block.dtype),
        compiler_params=pltpu.CompilerParams(vmem_limit_bytes=8 << 20),
        name="spread",
    )(block)


def shards(activations, out_grads, proj_in, proj_out, doc_ids, queries, block_owner):
    core0 = (lax.axis_index("tensor") & 1) == 0
    half = TOKENS // 2

    send, keep = project(out_grads, activations, proj_out.T, proj_in.T)
    total = keep + swap(send, 1, 1)
    total = total + swap(total, 2, 6)
    more = swap(total, 6, 2)

    columns = queries.shape[1] // 2
    mine, other = pick(core0, queries[:, :columns], queries[:, columns:])
    got = swap(other, 1, 1)

    ids = jnp.where(core0, doc_ids[:, :half], doc_ids[:, half:])
    here = lax.axis_index("dp")
    owner = lax.dynamic_slice(block_owner, (here,), (1,), allow_negative_indices=False)[0] & (N_DP - 1)
    more, mine, got, owner = lax.optimization_barrier((more, mine, got, owner))
    feat = features(ids, total, more).reshape(DOCS_DEV, 2, RANK // 2, RANK)
    keep, send = pick(core0, feat[:, 0], feat[:, 1])
    block = (keep + swap(send, 1, 1)).astype(jnp.bfloat16)
    block = block.reshape(DOCS_DEV, 2, columns // 2).transpose(1, 0, 2).reshape(2 * DOCS_DEV, columns // 2)

    feats = lax.all_to_all(spread(block), "dp", 0, 0).reshape(2 * DOCS, columns // 2)
    scored = score(mine, got, feats)
    rows = queries.shape[0]
    stored = (scored[:rows] + swap(scored[rows:], 1, 1)).astype(jnp.bfloat16)

    blocks = lax.all_to_all(spread(stored), "dp", 0, 0)
    picked = lax.dynamic_slice(blocks, (owner, 0, 0), (1,) + stored.shape, allow_negative_indices=False)
    return picked[0].astype(jnp.float32)


def solution(mesh):
    placed = (
        P("dp", "tensor"),
        P("dp", "tensor"),
        P("tensor", None),
        P("tensor", None),
        P("dp", None),
        P(("dp", "tensor"), None),
        P(),
    )
    return jax.shard_map(
        shards, mesh=mesh, in_specs=placed, out_specs=P(("dp", "tensor"), None), check_vma=False
    )
```

```python
import jax
import jax.numpy as jnp
from jax import lax
from jax.experimental import pallas as pl
from jax.experimental.pallas import tpu as pltpu
from jax.sharding import PartitionSpec as P

RANK = 64
DOCS_DEV = 4
N_DP = 32
DOCS = N_DP * DOCS_DEV
Y = 4
TOKENS = 1024
STEP = 256
NT = (((1,), (1,)), ((), ()))


def swap(value, even, odd):
    return lax.ppermute(value, "tensor", [(i, i ^ (odd if i & 1 else even)) for i in range(8)])


def pick(first, low, high):
    return jnp.where(first, low, high), jnp.where(first, high, low)


def token_block(ref, block):
    return ref.at[pl.ds(pl.multiple_of(block * STEP, STEP), STEP)]


def project_block(grads, acts, wide_out, wide_in, block, target):
    here = pl.ds(pl.multiple_of(block * STEP, STEP), STEP)
    target[here] = jnp.dot(grads[here], wide_out[...], preferred_element_type=jnp.float32) + jnp.dot(
        acts[here], wide_in[...], preferred_element_type=jnp.float32
    )


def project_sent_kernel(
    out_grads, activations, proj_out, proj_in, send, grads_kept, acts_kept, wide_out, wide_in, grads, acts, raw_out, raw_in, sem
):
    blocks = TOKENS // STEP // 2
    core = lax.axis_index("tensor") & 1

    def copies(half, block, to_grads, to_acts, base):
        return (
            pltpu.make_async_copy(
                token_block(out_grads, half * blocks + block), token_block(to_grads, block), sem.at[base + 2 * block]
            ),
            pltpu.make_async_copy(
                token_block(activations, half * blocks + block), token_block(to_acts, block), sem.at[base + 2 * block + 1]
            ),
        )

    weights = (
        pltpu.make_async_copy(proj_out, raw_out, sem.at[0]),
        pltpu.make_async_copy(proj_in, raw_in, sem.at[1]),
    )
    later = [copy for block in range(blocks) for copy in copies(core, block, grads_kept, acts_kept, 2 + 2 * blocks)]
    for copy in weights:
        copy.start()
    for block in range(blocks):
        for copy in copies(1 - core, block, grads, acts, 2):
            copy.start()
    for copy in later:
        copy.start()
    for copy in weights:
        copy.wait()
    wide_out[...] = jnp.concatenate([raw_out[...], jnp.zeros_like(raw_out)], axis=0).T
    wide_in[...] = jnp.concatenate([jnp.zeros_like(raw_in), raw_in[...]], axis=0).T

    @pl.loop(0, blocks)
    def _(block):
        for copy in copies(1 - core, block, grads, acts, 2):
            copy.wait()
        project_block(grads, acts, wide_out, wide_in, block, send)

    for copy in later:
        copy.wait()


def project_kept_kernel(grads, acts, wide_out, wide_in, keep):
    @pl.loop(0, TOKENS // STEP // 2)
    def _(block):
        project_block(grads, acts, wide_out, wide_in, block, keep)


def project(out_grads, activations, proj_out, proj_in, meanwhile):
    d, ff = out_grads.shape[1], activations.shape[1]
    half = TOKENS // 2
    in_vmem, in_hbm = pl.BlockSpec(memory_space=pltpu.VMEM), pl.BlockSpec(memory_space=pltpu.HBM)
    args = [pltpu.with_memory_space_constraint(x, pltpu.HBM) for x in (out_grads, activations, proj_out, proj_in)]
    send, *rest = pl.pallas_call(
        project_sent_kernel,
        in_specs=[in_hbm] * 4,
        out_specs=[in_vmem] * 5,
        out_shape=[
            pltpu.VMEM((half, 2 * RANK), jnp.float32),
            pltpu.VMEM((half, d), jnp.bfloat16),
            pltpu.VMEM((half, ff), jnp.bfloat16),
            pltpu.VMEM((d, 2 * RANK), jnp.bfloat16),
            pltpu.VMEM((ff, 2 * RANK), jnp.bfloat16),
        ],
        scratch_shapes=[
            pltpu.VMEM((half, d), jnp.bfloat16),
            pltpu.VMEM((half, ff), jnp.bfloat16),
            pltpu.VMEM((RANK, d), jnp.bfloat16),
            pltpu.VMEM((RANK, ff), jnp.bfloat16),
            pltpu.SemaphoreType.DMA((2 + 2 * (TOKENS // STEP),)),
        ],
        compiler_params=pltpu.CompilerParams(vmem_limit_bytes=24 << 20),
        name="project_sent",
    )(*args)
    got = meanwhile(send)
    keep = pl.pallas_call(
        project_kept_kernel,
        in_specs=[in_vmem] * 4,
        out_specs=in_vmem,
        out_shape=pltpu.VMEM((half, 2 * RANK), jnp.float32),
        compiler_params=pltpu.CompilerParams(vmem_limit_bytes=24 << 20),
        cost_estimate=pl.CostEstimate(
            flops=2 * half * (d + ff) * 2 * RANK, bytes_accessed=2 * half * (d + ff), transcendentals=0
        ),
        name="project_kept",
    )(*rest)
    return keep, got


def features_kernel(ids, total, more, feat):
    both = total[...] + more[...]
    out_t = both.T[:RANK]
    weighted = jnp.concatenate([jnp.where(ids[...] == d, out_t, 0.0) for d in range(DOCS_DEV)], axis=0)
    feat[...] = jnp.dot(
        weighted, both[:, RANK:], precision=lax.Precision.HIGHEST, preferred_element_type=jnp.float32
    )


def features(ids, total, more):
    return pl.pallas_call(
        features_kernel,
        out_shape=jax.ShapeDtypeStruct((DOCS_DEV * RANK, RANK), jnp.float32),
        compiler_params=pltpu.CompilerParams(vmem_limit_bytes=16 << 20),
        name="features",
    )(ids, total, more)


def score_kernel(feats, *refs):
    queries, (keep, send, rows) = refs[:-3], refs[-3:]
    half, count = feats.shape[1], feats.shape[0] // 2
    each = queries[0].shape[1]
    here = lax.axis_index("dp") & (Y - 1)
    for step, q in enumerate(queries):
        for h in range(2):
            for core in range(2):
                start = ((2 * h + core) * Y + (here ^ step)) * each
                rows[pl.ds(pl.multiple_of(start, each), each)] = q[core, :, h * half : (h + 1) * half]
    every = lax.dot_general(feats[...], rows[...], NT, preferred_element_type=jnp.float32)
    doc = lax.broadcasted_iota(jnp.int32, (count, 2 * count), 0)
    source = lax.broadcasted_iota(jnp.int32, (count, 2 * count), 1)
    first = (doc >> 2) * 8 + (doc & 3)
    width = rows.shape[0] // 2
    scored = jnp.dot(
        (source == first).astype(jnp.float32), every[:, :width], precision=lax.Precision.HIGHEST,
        preferred_element_type=jnp.float32,
    ) + jnp.dot(
        (source == first + 4).astype(jnp.float32), every[:, width:], precision=lax.Precision.HIGHEST,
        preferred_element_type=jnp.float32,
    )
    keep[...] = scored[:, : width // 2]
    send[...] = scored[:, width // 2 :]


def score(feats, queries):
    out = jax.ShapeDtypeStruct((feats.shape[0] // 2, len(queries) * queries[0].shape[1]), jnp.float32)
    return pl.pallas_call(
        score_kernel,
        out_shape=[out, out],
        scratch_shapes=[pltpu.VMEM((4 * len(queries) * queries[0].shape[1], feats.shape[1]), feats.dtype)],
        compiler_params=pltpu.CompilerParams(vmem_limit_bytes=16 << 20),
        name="score",
    )(feats, *queries)


def place_kernel(owner, blocks, scores, wide):
    lanes, rows = blocks.shape[2], scores.shape[0]
    block = owner[0]
    line = blocks[pl.ds(block & ~(Y - 1), Y)].reshape(DOCS, lanes)
    row = lax.broadcasted_iota(jnp.int32, (DOCS, DOCS), 0)
    column = lax.broadcasted_iota(jnp.int32, (DOCS, DOCS), 1)
    spot = column == ((row >> 2) & 7) * 16 + (row >> 5) * 4 + (row & 3)
    wide[...] = lax.dot_general(
        line, spot.astype(line.dtype), (((0,), (0,)), ((), ())), preferred_element_type=jnp.float32
    )
    scores[...] = wide[pl.ds(pl.multiple_of((block & (Y - 1)) * rows, rows), rows)]


def place(owner, blocks):
    rows = blocks.shape[2] // Y
    return pl.pallas_call(
        place_kernel,
        in_specs=[pl.BlockSpec(memory_space=pltpu.SMEM), pl.BlockSpec(memory_space=pltpu.VMEM)],
        out_specs=pl.BlockSpec(memory_space=pltpu.VMEM),
        out_shape=jax.ShapeDtypeStruct((rows, DOCS), jnp.float32),
        scratch_shapes=[pltpu.VMEM((blocks.shape[2], DOCS), jnp.float32)],
        compiler_params=pltpu.CompilerParams(vmem_limit_bytes=16 << 20),
        name="place",
    )(owner, blocks)


def spread_kernel(block, everyone):
    everyone[...] = jnp.broadcast_to(block[...], everyone.shape)


def spread(block, peers):
    return pl.pallas_call(
        spread_kernel,
        out_specs=pl.BlockSpec(memory_space=pltpu.VMEM),
        out_shape=pltpu.VMEM((peers,) + block.shape, block.dtype),
        compiler_params=pltpu.CompilerParams(vmem_limit_bytes=8 << 20),
        name="spread",
    )(block)


def shards(activations, out_grads, proj_in, proj_out, doc_ids, queries, block_owner):
    core0 = (lax.axis_index("tensor") & 1) == 0
    half = TOKENS // 2
    core0, proj_in = lax.optimization_barrier((core0, proj_in))

    keep, got = project(out_grads, activations, proj_out.T, proj_in.T, lambda send: swap(send, 1, 1))
    total = keep + got
    total = total + swap(total, 2, 6)
    more = swap(total, 6, 2)

    columns = queries.shape[1] // 2
    mine, other = pick(core0, queries[:, :columns], queries[:, columns:])
    lines = [jnp.stack([mine, swap(other, 1, 1)])]
    lines += [lax.ppermute(lines[0], "dp", [(i, i ^ step) for i in range(N_DP)]) for step in range(1, Y)]

    ids = jnp.where(core0, doc_ids[:, :half], doc_ids[:, half:])
    here = lax.axis_index("dp")
    owner = lax.dynamic_slice(block_owner, (here,), (1,), allow_negative_indices=False)
    more, lines, owner = lax.optimization_barrier((more, lines, owner))
    feat = features(ids, total, more).reshape(DOCS_DEV, 2, RANK // 2, RANK)
    keep, send = pick(core0, feat[:, 0], feat[:, 1])
    block = (keep + swap(send, 1, 1)).astype(jnp.bfloat16)
    block = block.reshape(DOCS_DEV, 2, columns // 2).transpose(1, 0, 2).reshape(2 * DOCS_DEV, columns // 2)

    peers = N_DP // Y
    groups = [[g * Y + y for g in range(peers)] for y in range(Y)]
    feats = lax.all_to_all(spread(block, peers), "dp", 0, 0, axis_index_groups=groups)
    keep, send = score(feats.reshape(peers * 2 * DOCS_DEV, columns // 2), lines)
    stored = (keep + swap(send, 1, 1)).astype(jnp.bfloat16)

    return place(owner, lax.all_to_all(spread(stored, N_DP), "dp", 0, 0))


def solution(mesh):
    placed = (
        P("dp", "tensor"),
        P("dp", "tensor"),
        P("tensor", None),
        P("tensor", None),
        P("dp", None),
        P(("dp", "tensor"), None),
        P(),
    )
    return jax.shard_map(
        shards, mesh=mesh, in_specs=placed, out_specs=P(("dp", "tensor"), None), check_vma=False
    )
```

```python
import jax
import jax.numpy as jnp
from jax import lax
from jax.experimental import pallas as pl
from jax.experimental.pallas import tpu as pltpu
from jax.sharding import PartitionSpec as P

RANK = 64
DOCS_DEV = 4
N_DP = 32
DOCS = N_DP * DOCS_DEV
Y = 4
TOKENS = 1024
STEP = 256
NT = (((1,), (1,)), ((), ()))


def swap(value, even, odd):
    return lax.ppermute(value, "tensor", [(i, i ^ (odd if i & 1 else even)) for i in range(8)])


def token_block(ref, block):
    return ref.at[pl.ds(pl.multiple_of(block * STEP, STEP), STEP)]


def project_block(grads, acts, wide_out, wide_in, block, target):
    here = pl.ds(pl.multiple_of(block * STEP, STEP), STEP)
    target[here] = jnp.dot(grads[here], wide_out[...], preferred_element_type=jnp.float32) + jnp.dot(
        acts[here], wide_in[...], preferred_element_type=jnp.float32
    )


def project_sent_kernel(
    out_grads, activations, proj_out, proj_in, send, grads_kept, acts_kept, wide_out, wide_in, grads, acts, raw_out, raw_in, sem
):
    blocks = TOKENS // STEP // 2
    core = lax.axis_index("tensor") & 1

    def copies(half, block, to_grads, to_acts, base):
        return (
            pltpu.make_async_copy(
                token_block(out_grads, half * blocks + block), token_block(to_grads, block), sem.at[base + 2 * block]
            ),
            pltpu.make_async_copy(
                token_block(activations, half * blocks + block), token_block(to_acts, block), sem.at[base + 2 * block + 1]
            ),
        )

    weights = (
        pltpu.make_async_copy(proj_out, raw_out, sem.at[0]),
        pltpu.make_async_copy(proj_in, raw_in, sem.at[1]),
    )
    later = [copy for block in range(blocks) for copy in copies(core, block, grads_kept, acts_kept, 2 + 2 * blocks)]
    for copy in weights:
        copy.start()
    for block in range(blocks):
        for copy in copies(1 - core, block, grads, acts, 2):
            copy.start()
    for copy in later:
        copy.start()
    for copy in weights:
        copy.wait()
    wide_out[...] = jnp.concatenate([raw_out[...], jnp.zeros_like(raw_out)], axis=0).T
    wide_in[...] = jnp.concatenate([jnp.zeros_like(raw_in), raw_in[...]], axis=0).T

    @pl.loop(0, blocks)
    def _(block):
        for copy in copies(1 - core, block, grads, acts, 2):
            copy.wait()
        project_block(grads, acts, wide_out, wide_in, block, send)

    for copy in later:
        copy.wait()


def project_kept_kernel(grads, acts, wide_out, wide_in, keep):
    @pl.loop(0, TOKENS // STEP // 2)
    def _(block):
        project_block(grads, acts, wide_out, wide_in, block, keep)


def project(out_grads, activations, proj_out, proj_in, meanwhile):
    d, ff = out_grads.shape[1], activations.shape[1]
    half = TOKENS // 2
    in_vmem, in_hbm = pl.BlockSpec(memory_space=pltpu.VMEM), pl.BlockSpec(memory_space=pltpu.HBM)
    args = [pltpu.with_memory_space_constraint(x, pltpu.HBM) for x in (out_grads, activations, proj_out, proj_in)]
    send, *rest = pl.pallas_call(
        project_sent_kernel,
        in_specs=[in_hbm] * 4,
        out_specs=[in_vmem] * 5,
        out_shape=[
            pltpu.VMEM((half, 2 * RANK), jnp.float32),
            pltpu.VMEM((half, d), jnp.bfloat16),
            pltpu.VMEM((half, ff), jnp.bfloat16),
            pltpu.VMEM((d, 2 * RANK), jnp.bfloat16),
            pltpu.VMEM((ff, 2 * RANK), jnp.bfloat16),
        ],
        scratch_shapes=[
            pltpu.VMEM((half, d), jnp.bfloat16),
            pltpu.VMEM((half, ff), jnp.bfloat16),
            pltpu.VMEM((RANK, d), jnp.bfloat16),
            pltpu.VMEM((RANK, ff), jnp.bfloat16),
            pltpu.SemaphoreType.DMA((2 + 2 * (TOKENS // STEP),)),
        ],
        compiler_params=pltpu.CompilerParams(vmem_limit_bytes=24 << 20),
        name="project_sent",
    )(*args)
    got = meanwhile(send)
    keep = pl.pallas_call(
        project_kept_kernel,
        in_specs=[in_vmem] * 4,
        out_specs=in_vmem,
        out_shape=pltpu.VMEM((half, 2 * RANK), jnp.float32),
        compiler_params=pltpu.CompilerParams(vmem_limit_bytes=24 << 20),
        cost_estimate=pl.CostEstimate(
            flops=2 * half * (d + ff) * 2 * RANK, bytes_accessed=2 * half * (d + ff), transcendentals=0
        ),
        name="project_kept",
    )(*rest)
    return keep, got


def features_kernel(ids, total, more, feat):
    both = total[...] + more[...]
    out_t = both.T[:RANK]
    weighted = jnp.concatenate([jnp.where(ids[...] == d, out_t, 0.0) for d in range(DOCS_DEV)], axis=0)
    feat[...] = jnp.dot(
        weighted, both[:, RANK:], precision=lax.Precision.HIGHEST, preferred_element_type=jnp.float32
    )


def features(ids, total, more):
    return pl.pallas_call(
        features_kernel,
        out_shape=jax.ShapeDtypeStruct((DOCS_DEV * RANK, RANK), jnp.float32),
        compiler_params=pltpu.CompilerParams(vmem_limit_bytes=16 << 20),
        name="features",
    )(ids, total, more)


def score_kernel(feats, *refs):
    queries, (everyone, rows) = refs[:-2], refs[-2:]
    half, count = feats.shape[1], feats.shape[0] // 2
    each = queries[0].shape[0]
    here = lax.axis_index("dp") & (Y - 1)
    for step, q in enumerate(queries):
        for h in range(2):
            start = (h * Y + (here ^ step)) * each
            rows[pl.ds(pl.multiple_of(start, each), each)] = q[:, h * half : (h + 1) * half]
    every = lax.dot_general(feats[...], rows[...], NT, preferred_element_type=jnp.float32)
    doc = lax.broadcasted_iota(jnp.int32, (count, 2 * count), 0)
    source = lax.broadcasted_iota(jnp.int32, (count, 2 * count), 1)
    first = (doc >> 2) * 8 + (doc & 3)
    width = rows.shape[0] // 2
    scored = jnp.dot(
        (source == first).astype(jnp.float32), every[:, :width], precision=lax.Precision.HIGHEST,
        preferred_element_type=jnp.float32,
    ) + jnp.dot(
        (source == first + 4).astype(jnp.float32), every[:, width:], precision=lax.Precision.HIGHEST,
        preferred_element_type=jnp.float32,
    )
    everyone[...] = jnp.broadcast_to(scored.astype(everyone.dtype), everyone.shape)


def score(feats, queries):
    docs, rows = feats.shape[0] // 2, len(queries) * queries[0].shape[0]
    return pl.pallas_call(
        score_kernel,
        out_specs=pl.BlockSpec(memory_space=pltpu.VMEM),
        out_shape=pltpu.VMEM((N_DP, docs, rows), jnp.bfloat16),
        scratch_shapes=[pltpu.VMEM((2 * rows, feats.shape[1]), feats.dtype)],
        compiler_params=pltpu.CompilerParams(vmem_limit_bytes=16 << 20),
        name="score",
    )(feats, *queries)


def place_kernel(owners, blocks, scores):
    lanes, rows = blocks.shape[2], scores.shape[0]
    here = lax.broadcasted_iota(jnp.int32, owners.shape, 1) == lax.axis_index("dp")
    owner = jnp.sum(jnp.where(here, owners[...], 0), axis=1, keepdims=True)
    line = jnp.zeros((DOCS, lanes), jnp.float32)
    for first in range(0, N_DP, Y):
        chosen = (owner & ~(Y - 1)) == first
        line = line + jnp.where(chosen, blocks[first : first + Y].reshape(DOCS, lanes).astype(jnp.float32), 0.0)
    row = lax.broadcasted_iota(jnp.int32, (DOCS, DOCS), 0)
    column = lax.broadcasted_iota(jnp.int32, (DOCS, DOCS), 1)
    spot = column == ((row >> 2) & 7) * 16 + (row >> 5) * 4 + (row & 3)
    wide = jnp.dot(line.T.astype(blocks.dtype), spot.astype(blocks.dtype), preferred_element_type=jnp.float32)
    total = jnp.zeros_like(scores)
    for y in range(Y):
        total = total + jnp.where((owner & (Y - 1)) == y, wide[y * rows : (y + 1) * rows], 0.0)
    scores[...] = total


def place(owners, blocks):
    return pl.pallas_call(
        place_kernel,
        out_shape=jax.ShapeDtypeStruct((blocks.shape[2] // Y, DOCS), jnp.float32),
        compiler_params=pltpu.CompilerParams(vmem_limit_bytes=16 << 20),
        name="place",
    )(owners, blocks)


def spread_kernel(block, everyone):
    everyone[...] = jnp.broadcast_to(block[...], everyone.shape)


def spread(block, peers):
    return pl.pallas_call(
        spread_kernel,
        out_specs=pl.BlockSpec(memory_space=pltpu.VMEM),
        out_shape=pltpu.VMEM((peers,) + block.shape, block.dtype),
        compiler_params=pltpu.CompilerParams(vmem_limit_bytes=8 << 20),
        name="spread",
    )(block)


def shards(activations, out_grads, proj_in, proj_out, doc_ids, queries, block_owner):
    core0 = (lax.axis_index("tensor") & 1) == 0
    half = TOKENS // 2
    core0, proj_in = lax.optimization_barrier((core0, proj_in))

    keep, got = project(out_grads, activations, proj_out.T, proj_in.T, lambda send: swap(send, 1, 1))
    total = keep + got
    total = total + swap(total, 2, 6)
    more = swap(total, 6, 2)

    lines = [queries] + [lax.ppermute(queries, "dp", [(i, i ^ step) for i in range(N_DP)]) for step in range(1, Y)]

    ids = jnp.where(core0, doc_ids[:, :half], doc_ids[:, half:])
    more, lines = lax.optimization_barrier((more, lines))
    feat = features(ids, total, more)
    block = (feat + swap(feat, 1, 1)).astype(jnp.bfloat16)
    block = block.reshape(DOCS_DEV, 2, RANK * RANK // 2).transpose(1, 0, 2).reshape(2 * DOCS_DEV, RANK * RANK // 2)

    peers = N_DP // Y
    groups = [[g * Y + y for g in range(peers)] for y in range(Y)]
    feats = lax.all_to_all(spread(block, peers), "dp", 0, 0, axis_index_groups=groups)
    blocks = score(feats.reshape(peers * 2 * DOCS_DEV, RANK * RANK // 2), lines)

    return place(block_owner.reshape(1, N_DP), lax.all_to_all(blocks, "dp", 0, 0))


def solution(mesh):
    placed = (
        P("dp", "tensor"),
        P("dp", "tensor"),
        P("tensor", None),
        P("tensor", None),
        P("dp", None),
        P(("dp", "tensor"), None),
        P(),
    )
    return jax.shard_map(
        shards, mesh=mesh, in_specs=placed, out_specs=P(("dp", "tensor"), None), check_vma=False
    )
```

```python
import jax
import jax.numpy as jnp
from jax import lax
from jax.experimental import pallas as pl
from jax.experimental.pallas import tpu as pltpu
from jax.sharding import PartitionSpec as P

RANK = 64
DOCS_DEV = 4
N_DP = 32
DOCS = N_DP * DOCS_DEV
Y = 4
TOKENS = 1024
STEP = 256
NT = (((1,), (1,)), ((), ()))


def swap(value, even, odd):
    return lax.ppermute(value, "tensor", [(i, i ^ (odd if i & 1 else even)) for i in range(8)])


def token_block(ref, block):
    return ref.at[pl.ds(pl.multiple_of(block * STEP, STEP), STEP)]


def project_block(grads, acts, wide_out, wide_in, block, target, place):
    here = pl.ds(pl.multiple_of(block * STEP, STEP), STEP)
    there = pl.ds(pl.multiple_of(place * STEP, STEP), STEP)
    target[there] = jnp.dot(grads[here], wide_out[...], preferred_element_type=jnp.float32) + jnp.dot(
        acts[here], wide_in[...], preferred_element_type=jnp.float32
    )


def project_early_kernel(
    out_grads, activations, proj_out, proj_in, send, first, grads_last, acts_last, wide_out, wide_in, grads, acts, raw_out, raw_in, sem
):
    blocks = TOKENS // STEP
    half = blocks // 2
    core = lax.axis_index("tensor") & 1

    def copies(block, to_grads, to_acts, place):
        which = jnp.where(block < half, (1 - core) * half, core * half - half) + block
        return (
            pltpu.make_async_copy(token_block(out_grads, which), token_block(to_grads, place), sem.at[2 + 2 * block]),
            pltpu.make_async_copy(token_block(activations, which), token_block(to_acts, place), sem.at[3 + 2 * block]),
        )

    weights = (
        pltpu.make_async_copy(proj_out, raw_out, sem.at[0]),
        pltpu.make_async_copy(proj_in, raw_in, sem.at[1]),
    )
    last = copies(blocks - 1, grads_last, acts_last, 0)
    for copy in weights:
        copy.start()
    for block in range(blocks - 1):
        for copy in copies(block, grads, acts, block):
            copy.start()
    for copy in last:
        copy.start()
    for copy in weights:
        copy.wait()
    wide_out[...] = jnp.concatenate([raw_out[...], jnp.zeros_like(raw_out)], axis=0).T
    wide_in[...] = jnp.concatenate([jnp.zeros_like(raw_in), raw_in[...]], axis=0).T

    @pl.loop(0, half)
    def _(block):
        for copy in copies(block, grads, acts, block):
            copy.wait()
        project_block(grads, acts, wide_out, wide_in, block, send, block)

    @pl.loop(half, blocks - 1)
    def _(block):
        for copy in copies(block, grads, acts, block):
            copy.wait()
        project_block(grads, acts, wide_out, wide_in, block, first, block - half)

    for copy in last:
        copy.wait()


def project_late_kernel(first, grads, acts, wide_out, wide_in, keep):
    keep[: first.shape[0]] = first[...]

    @pl.loop(0, 1)
    def _(block):
        project_block(grads, acts, wide_out, wide_in, block, keep, block + first.shape[0] // STEP)


def project(out_grads, activations, proj_out, proj_in, meanwhile):
    d, ff = out_grads.shape[1], activations.shape[1]
    half = TOKENS // 2
    in_vmem, in_hbm = pl.BlockSpec(memory_space=pltpu.VMEM), pl.BlockSpec(memory_space=pltpu.HBM)
    args = [pltpu.with_memory_space_constraint(x, pltpu.HBM) for x in (out_grads, activations, proj_out, proj_in)]
    send, *rest = pl.pallas_call(
        project_early_kernel,
        in_specs=[in_hbm] * 4,
        out_specs=[in_vmem] * 6,
        out_shape=[
            pltpu.VMEM((half, 2 * RANK), jnp.float32),
            pltpu.VMEM((half - STEP, 2 * RANK), jnp.float32),
            pltpu.VMEM((STEP, d), jnp.bfloat16),
            pltpu.VMEM((STEP, ff), jnp.bfloat16),
            pltpu.VMEM((d, 2 * RANK), jnp.bfloat16),
            pltpu.VMEM((ff, 2 * RANK), jnp.bfloat16),
        ],
        scratch_shapes=[
            pltpu.VMEM((TOKENS - STEP, d), jnp.bfloat16),
            pltpu.VMEM((TOKENS - STEP, ff), jnp.bfloat16),
            pltpu.VMEM((RANK, d), jnp.bfloat16),
            pltpu.VMEM((RANK, ff), jnp.bfloat16),
            pltpu.SemaphoreType.DMA((2 + 2 * (TOKENS // STEP),)),
        ],
        compiler_params=pltpu.CompilerParams(vmem_limit_bytes=24 << 20),
        name="project_early",
    )(*args)
    got = meanwhile(send)
    keep = pl.pallas_call(
        project_late_kernel,
        in_specs=[in_vmem] * 5,
        out_specs=in_vmem,
        out_shape=pltpu.VMEM((half, 2 * RANK), jnp.float32),
        compiler_params=pltpu.CompilerParams(vmem_limit_bytes=24 << 20),
        cost_estimate=pl.CostEstimate(
            flops=2 * half * (d + ff) * 2 * RANK, bytes_accessed=2 * half * (d + ff), transcendentals=0
        ),
        name="project_late",
    )(*rest)
    return keep, got


def features_kernel(ids, total, more, feat):
    both = total[...] + more[...]
    out_t = both.T[:RANK]
    weighted = jnp.concatenate([jnp.where(ids[...] == d, out_t, 0.0) for d in range(DOCS_DEV)], axis=0)
    feat[...] = jnp.dot(
        weighted, both[:, RANK:], precision=lax.Precision.HIGHEST, preferred_element_type=jnp.float32
    )


def features(ids, total, more):
    return pl.pallas_call(
        features_kernel,
        out_shape=jax.ShapeDtypeStruct((DOCS_DEV * RANK, RANK), jnp.float32),
        compiler_params=pltpu.CompilerParams(vmem_limit_bytes=16 << 20),
        name="features",
    )(ids, total, more)


def score_kernel(owners, feats, *refs):
    queries, (everyone, rows) = refs[:-2], refs[-2:]
    half, count = feats.shape[1], feats.shape[0] // 2
    each = queries[0].shape[0]
    here = lax.axis_index("dp") & (Y - 1)
    for step, q in enumerate(queries):
        for h in range(2):
            start = (h * Y + (here ^ step)) * each
            rows[pl.ds(pl.multiple_of(start, each), each)] = q[:, h * half : (h + 1) * half]
    every = lax.dot_general(feats[...], rows[...], NT, preferred_element_type=jnp.float32)
    doc = lax.broadcasted_iota(jnp.int32, (count, 2 * count), 0)
    source = lax.broadcasted_iota(jnp.int32, (count, 2 * count), 1)
    first = (doc >> 2) * 8 + (doc & 3)
    width = rows.shape[0] // 2
    scored = jnp.dot(
        (source == first).astype(jnp.float32), every[:, :width], precision=lax.Precision.HIGHEST,
        preferred_element_type=jnp.float32,
    ) + jnp.dot(
        (source == first + 4).astype(jnp.float32), every[:, width:], precision=lax.Precision.HIGHEST,
        preferred_element_type=jnp.float32,
    )
    scored = scored.astype(everyone.dtype).astype(jnp.float32)
    tiles = [scored[8 * x : 8 * x + 8] for x in range(count // 8)]
    lane = lax.broadcasted_iota(jnp.int32, tiles[0].shape, 1) >> 5
    packed = []
    for y in range(Y):
        total = jnp.zeros_like(tiles[0])
        for x, tile in enumerate(tiles):
            shift = (x - y) % Y * each
            total = jnp.where(lane == x, pltpu.roll(tile, shift, 1) if shift else tile, total)
        packed.append(total)
    for peer in range(N_DP):
        y = owners[:, peer : peer + 1] & (Y - 1)
        chosen = jnp.where(y < 2, jnp.where(y == 0, packed[0], packed[1]), jnp.where(y == 2, packed[2], packed[3]))
        everyone[peer] = chosen.astype(everyone.dtype)


def score(owners, feats, queries):
    rows = len(queries) * queries[0].shape[0]
    return pl.pallas_call(
        score_kernel,
        out_specs=pl.BlockSpec(memory_space=pltpu.VMEM),
        out_shape=pltpu.VMEM((N_DP, 8, 128), jnp.bfloat16),
        scratch_shapes=[pltpu.VMEM((2 * rows, feats.shape[1]), feats.dtype)],
        compiler_params=pltpu.CompilerParams(vmem_limit_bytes=16 << 20),
        name="score",
    )(owners, feats, *queries)


def place_kernel(owners, blocks, scores):
    rows = scores.shape[0]
    here = lax.broadcasted_iota(jnp.int32, owners.shape, 1) == lax.axis_index("dp")
    owner = jnp.sum(jnp.where(here, owners[...], 0), axis=1, keepdims=True)
    line = jnp.zeros((Y * 8, blocks.shape[2]), jnp.float32)
    for first in range(0, N_DP, Y):
        chosen = (owner & ~(Y - 1)) == first
        line = line + jnp.where(chosen, blocks[first : first + Y].astype(jnp.float32).reshape(line.shape), 0.0)
    line = line.T.astype(blocks.dtype)
    row = lax.broadcasted_iota(jnp.int32, (Y * 8, DOCS), 0)
    column = lax.broadcasted_iota(jnp.int32, (Y * 8, DOCS), 1)
    spot = ((row >> 2) & 1) * 16 + (row >> 3) * 4 + (row & 3)
    total = jnp.zeros_like(scores)
    for x in range(DOCS // 32):
        total = total + jnp.dot(
            line[x * rows : (x + 1) * rows], (column == spot + 32 * x).astype(line.dtype),
            preferred_element_type=jnp.float32,
        )
    scores[...] = total


def place(owners, blocks):
    return pl.pallas_call(
        place_kernel,
        out_shape=jax.ShapeDtypeStruct((32, DOCS), jnp.float32),
        compiler_params=pltpu.CompilerParams(vmem_limit_bytes=16 << 20),
        name="place",
    )(owners, blocks)


def spread_kernel(block, everyone):
    everyone[...] = jnp.broadcast_to(block[...], everyone.shape)


def spread(block, peers):
    return pl.pallas_call(
        spread_kernel,
        out_specs=pl.BlockSpec(memory_space=pltpu.VMEM),
        out_shape=pltpu.VMEM((peers,) + block.shape, block.dtype),
        compiler_params=pltpu.CompilerParams(vmem_limit_bytes=8 << 20),
        name="spread",
    )(block)


def shards(activations, out_grads, proj_in, proj_out, doc_ids, queries, block_owner):
    core0 = (lax.axis_index("tensor") & 1) == 0
    half = TOKENS // 2
    core0, proj_in = lax.optimization_barrier((core0, proj_in))

    keep, got = project(out_grads, activations, proj_out.T, proj_in.T, lambda send: swap(send, 1, 1))
    total = keep + got
    total = total + swap(total, 2, 6)
    more = swap(total, 6, 2)

    lines = [queries] + [lax.ppermute(queries, "dp", [(i, i ^ step) for i in range(N_DP)]) for step in range(1, Y)]

    ids = jnp.where(core0, doc_ids[:, :half], doc_ids[:, half:])
    more, lines = lax.optimization_barrier((more, lines))
    feat = features(ids, total, more)
    block = (feat + swap(feat, 1, 1)).astype(jnp.bfloat16)
    block = block.reshape(DOCS_DEV, 2, RANK * RANK // 2).transpose(1, 0, 2).reshape(2 * DOCS_DEV, RANK * RANK // 2)

    peers = N_DP // Y
    groups = [[g * Y + y for g in range(peers)] for y in range(Y)]
    feats = lax.all_to_all(spread(block, peers), "dp", 0, 0, axis_index_groups=groups)
    owners = block_owner.reshape(1, N_DP)
    blocks = score(owners, feats.reshape(peers * 2 * DOCS_DEV, RANK * RANK // 2), lines)

    return place(owners, lax.all_to_all(blocks, "dp", 0, 0))


def solution(mesh):
    placed = (
        P("dp", "tensor"),
        P("dp", "tensor"),
        P("tensor", None),
        P("tensor", None),
        P("dp", None),
        P(("dp", "tensor"), None),
        P(),
    )
    return jax.shard_map(
        shards, mesh=mesh, in_specs=placed, out_specs=P(("dp", "tensor"), None), check_vma=False
    )
```

```python
import jax
import jax.numpy as jnp
from jax import lax
from jax.experimental import pallas as pl
from jax.experimental.pallas import tpu as pltpu
from jax.sharding import PartitionSpec as P

RANK = 64
DOCS_DEV = 4
N_DP = 32
DOCS = N_DP * DOCS_DEV
Y = 4
TOKENS = 1024
STEP = 256
NT = (((1,), (1,)), ((), ()))


def swap(value, even, odd):
    return lax.ppermute(value, "tensor", [(i, i ^ (odd if i & 1 else even)) for i in range(8)])


def token_block(ref, block):
    return ref.at[pl.ds(pl.multiple_of(block * STEP, STEP), STEP)]


def project_block(grads, acts, wide_out, wide_in, block, target, place):
    here = pl.ds(pl.multiple_of(block * STEP, STEP), STEP)
    there = pl.ds(pl.multiple_of(place * STEP, STEP), STEP)
    target[there] = jnp.dot(grads[here], wide_out[...], preferred_element_type=jnp.float32) + jnp.dot(
        acts[here], wide_in[...], preferred_element_type=jnp.float32
    )


def project_early_kernel(
    out_grads, activations, proj_out, proj_in, send, first, grads_last, acts_last, wide_out, wide_in, grads, acts, raw_out, raw_in, sem
):
    blocks = TOKENS // STEP
    half = blocks // 2
    core = lax.axis_index("tensor") & 1

    def copies(block, to_grads, to_acts, place):
        which = jnp.where(block < half, (1 - core) * half, core * half - half) + block
        return (
            pltpu.make_async_copy(token_block(out_grads, which), token_block(to_grads, place), sem.at[2 + 2 * block]),
            pltpu.make_async_copy(token_block(activations, which), token_block(to_acts, place), sem.at[3 + 2 * block]),
        )

    weights = (
        pltpu.make_async_copy(proj_out, raw_out, sem.at[0]),
        pltpu.make_async_copy(proj_in, raw_in, sem.at[1]),
    )
    last = copies(blocks - 1, grads_last, acts_last, 0)
    for copy in weights:
        copy.start()
    for block in range(blocks - 1):
        for copy in copies(block, grads, acts, block):
            copy.start()
    for copy in last:
        copy.start()
    for copy in weights:
        copy.wait()
    wide_out[...] = jnp.concatenate([raw_out[...], jnp.zeros_like(raw_out)], axis=0).T
    wide_in[...] = jnp.concatenate([jnp.zeros_like(raw_in), raw_in[...]], axis=0).T

    @pl.loop(0, half)
    def _(block):
        for copy in copies(block, grads, acts, block):
            copy.wait()
        project_block(grads, acts, wide_out, wide_in, block, send, block)

    @pl.loop(half, blocks - 1)
    def _(block):
        for copy in copies(block, grads, acts, block):
            copy.wait()
        project_block(grads, acts, wide_out, wide_in, block, first, block - half)

    for copy in last:
        copy.wait()


def project_late_kernel(first, grads, acts, wide_out, wide_in, keep):
    keep[: first.shape[0]] = first[...]

    @pl.loop(0, 1)
    def _(block):
        project_block(grads, acts, wide_out, wide_in, block, keep, block + first.shape[0] // STEP)


def project(out_grads, activations, proj_out, proj_in, meanwhile):
    d, ff = out_grads.shape[1], activations.shape[1]
    half = TOKENS // 2
    in_vmem, in_hbm = pl.BlockSpec(memory_space=pltpu.VMEM), pl.BlockSpec(memory_space=pltpu.HBM)
    args = [pltpu.with_memory_space_constraint(x, pltpu.HBM) for x in (out_grads, activations, proj_out, proj_in)]
    send, *rest = pl.pallas_call(
        project_early_kernel,
        in_specs=[in_hbm] * 4,
        out_specs=[in_vmem] * 6,
        out_shape=[
            pltpu.VMEM((half, 2 * RANK), jnp.float32),
            pltpu.VMEM((half - STEP, 2 * RANK), jnp.float32),
            pltpu.VMEM((STEP, d), jnp.bfloat16),
            pltpu.VMEM((STEP, ff), jnp.bfloat16),
            pltpu.VMEM((d, 2 * RANK), jnp.bfloat16),
            pltpu.VMEM((ff, 2 * RANK), jnp.bfloat16),
        ],
        scratch_shapes=[
            pltpu.VMEM((TOKENS - STEP, d), jnp.bfloat16),
            pltpu.VMEM((TOKENS - STEP, ff), jnp.bfloat16),
            pltpu.VMEM((RANK, d), jnp.bfloat16),
            pltpu.VMEM((RANK, ff), jnp.bfloat16),
            pltpu.SemaphoreType.DMA((2 + 2 * (TOKENS // STEP),)),
        ],
        compiler_params=pltpu.CompilerParams(vmem_limit_bytes=24 << 20),
        name="project_early",
    )(*args)
    got = meanwhile(send)
    keep = pl.pallas_call(
        project_late_kernel,
        in_specs=[in_vmem] * 5,
        out_specs=in_vmem,
        out_shape=pltpu.VMEM((half, 2 * RANK), jnp.float32),
        compiler_params=pltpu.CompilerParams(vmem_limit_bytes=24 << 20),
        cost_estimate=pl.CostEstimate(
            flops=2 * half * (d + ff) * 2 * RANK, bytes_accessed=2 * half * (d + ff), transcendentals=0
        ),
        name="project_late",
    )(*rest)
    return keep, got


def thirds(value):
    high = value.astype(jnp.bfloat16)
    rest = value - high.astype(jnp.float32)
    middle = rest.astype(jnp.bfloat16)
    return high, middle, (rest - middle.astype(jnp.float32)).astype(jnp.bfloat16)


def features_kernel(ids, total, more, feat):
    parts = thirds(total[...] + more[...])
    right = jnp.concatenate([part[:, RANK:] for part in parts], axis=1)

    def by_document(part):
        out_t = part.T[:RANK]
        return jnp.concatenate([jnp.where(ids[...] == d, out_t, jnp.zeros_like(out_t)) for d in range(DOCS_DEV)], axis=0)

    high, middle, low = [
        jnp.dot(by_document(part), right[:, : (3 - i) * RANK], preferred_element_type=jnp.float32)
        for i, part in enumerate(parts)
    ]
    least = (low + high[:, 2 * RANK :]) + middle[:, RANK:]
    feat[...] = least + ((middle[:, :RANK] + high[:, RANK : 2 * RANK]) + high[:, :RANK])


def features(ids, total, more):
    return pl.pallas_call(
        features_kernel,
        out_shape=jax.ShapeDtypeStruct((DOCS_DEV * RANK, RANK), jnp.float32),
        compiler_params=pltpu.CompilerParams(vmem_limit_bytes=16 << 20),
        name="features",
    )(ids, total, more)


def score_kernel(owners, feats, *refs):
    queries, (everyone, rows) = refs[:-2], refs[-2:]
    half, count = feats.shape[1], feats.shape[0] // 2
    each = queries[0].shape[0]
    here = lax.axis_index("dp") & (Y - 1)
    for step, q in enumerate(queries):
        for h in range(2):
            start = (h * Y + (here ^ step)) * each
            rows[pl.ds(pl.multiple_of(start, each), each)] = q[:, h * half : (h + 1) * half]
    every = lax.dot_general(feats[...], rows[...], NT, preferred_element_type=jnp.float32)
    width = rows.shape[0] // 2
    halves = jnp.concatenate([every[:, :width], every[:, width:]], axis=0)
    doc = lax.broadcasted_iota(jnp.int32, (count, 4 * count), 0)
    source = lax.broadcasted_iota(jnp.int32, (count, 4 * count), 1)
    first = (doc >> 2) * 8 + (doc & 3)
    spot = (source == first) | (source == first + 2 * count + 4)
    scored = jnp.dot(
        spot.astype(feats.dtype), jnp.concatenate(thirds(halves), axis=1), preferred_element_type=jnp.float32
    )
    scored = (scored[:, 2 * width :] + scored[:, width : 2 * width]) + scored[:, :width]
    scored = scored.astype(everyone.dtype).astype(jnp.float32)
    tiles = [scored[8 * x : 8 * x + 8] for x in range(count // 8)]
    lane = lax.broadcasted_iota(jnp.int32, tiles[0].shape, 1) >> 5
    packed = []
    for y in range(Y):
        total = jnp.zeros_like(tiles[0])
        for x, tile in enumerate(tiles):
            shift = (x - y) % Y * each
            total = jnp.where(lane == x, pltpu.roll(tile, shift, 1) if shift else tile, total)
        packed.append(total)
    for peer in range(N_DP):
        y = owners[:, peer : peer + 1] & (Y - 1)
        chosen = jnp.where(y < 2, jnp.where(y == 0, packed[0], packed[1]), jnp.where(y == 2, packed[2], packed[3]))
        everyone[peer] = chosen.astype(everyone.dtype)


def score(owners, feats, queries):
    rows = len(queries) * queries[0].shape[0]
    return pl.pallas_call(
        score_kernel,
        out_specs=pl.BlockSpec(memory_space=pltpu.VMEM),
        out_shape=pltpu.VMEM((N_DP, 8, 128), jnp.bfloat16),
        scratch_shapes=[pltpu.VMEM((2 * rows, feats.shape[1]), feats.dtype)],
        compiler_params=pltpu.CompilerParams(vmem_limit_bytes=16 << 20),
        name="score",
    )(owners, feats, *queries)


def place_kernel(owners, blocks, scores):
    rows = scores.shape[0]
    here = lax.broadcasted_iota(jnp.int32, owners.shape, 1) == lax.axis_index("dp")
    owner = jnp.sum(jnp.where(here, owners[...], 0), axis=1, keepdims=True)
    line = jnp.zeros((Y * 8, blocks.shape[2]), jnp.float32)
    for first in range(0, N_DP, Y):
        chosen = (owner & ~(Y - 1)) == first
        line = line + jnp.where(chosen, blocks[first : first + Y].astype(jnp.float32).reshape(line.shape), 0.0)
    line = line.T.astype(blocks.dtype)
    row = lax.broadcasted_iota(jnp.int32, (Y * 8, DOCS), 0)
    column = lax.broadcasted_iota(jnp.int32, (Y * 8, DOCS), 1)
    spot = ((row >> 2) & 1) * 16 + (row >> 3) * 4 + (row & 3)
    total = jnp.zeros_like(scores)
    for x in range(DOCS // 32):
        total = total + jnp.dot(
            line[x * rows : (x + 1) * rows], (column == spot + 32 * x).astype(line.dtype),
            preferred_element_type=jnp.float32,
        )
    scores[...] = total


def place(owners, blocks):
    return pl.pallas_call(
        place_kernel,
        out_shape=jax.ShapeDtypeStruct((32, DOCS), jnp.float32),
        compiler_params=pltpu.CompilerParams(vmem_limit_bytes=16 << 20),
        name="place",
    )(owners, blocks)


def spread_kernel(block, everyone):
    everyone[...] = jnp.broadcast_to(block[...], everyone.shape)


def spread(block, peers):
    return pl.pallas_call(
        spread_kernel,
        out_specs=pl.BlockSpec(memory_space=pltpu.VMEM),
        out_shape=pltpu.VMEM((peers,) + block.shape, block.dtype),
        compiler_params=pltpu.CompilerParams(vmem_limit_bytes=8 << 20),
        name="spread",
    )(block)


def shards(activations, out_grads, proj_in, proj_out, doc_ids, queries, block_owner):
    core0 = (lax.axis_index("tensor") & 1) == 0
    half = TOKENS // 2
    core0, proj_in = lax.optimization_barrier((core0, proj_in))

    keep, got = project(out_grads, activations, proj_out.T, proj_in.T, lambda send: swap(send, 1, 1))
    total = keep + got
    total = total + swap(total, 2, 6)
    more = swap(total, 6, 2)

    lines = [queries] + [lax.ppermute(queries, "dp", [(i, i ^ step) for i in range(N_DP)]) for step in range(1, Y)]

    ids = jnp.where(core0, doc_ids[:, :half], doc_ids[:, half:])
    more, lines = lax.optimization_barrier((more, lines))
    feat = features(ids, total, more)
    block = (feat + swap(feat, 1, 1)).astype(jnp.bfloat16)
    block = block.reshape(DOCS_DEV, 2, RANK * RANK // 2).transpose(1, 0, 2).reshape(2 * DOCS_DEV, RANK * RANK // 2)

    peers = N_DP // Y
    groups = [[g * Y + y for g in range(peers)] for y in range(Y)]
    feats = lax.all_to_all(spread(block, peers), "dp", 0, 0, axis_index_groups=groups)
    owners = block_owner.reshape(1, N_DP)
    blocks = score(owners, feats.reshape(peers * 2 * DOCS_DEV, RANK * RANK // 2), lines)

    return place(owners, lax.all_to_all(blocks, "dp", 0, 0))


def solution(mesh):
    placed = (
        P("dp", "tensor"),
        P("dp", "tensor"),
        P("tensor", None),
        P("tensor", None),
        P("dp", None),
        P(("dp", "tensor"), None),
        P(),
    )
    return jax.shard_map(
        shards, mesh=mesh, in_specs=placed, out_specs=P(("dp", "tensor"), None), check_vma=False
    )
```

```python
import jax
import jax.numpy as jnp
from jax import lax
from jax.experimental import pallas as pl
from jax.experimental.pallas import tpu as pltpu
from jax.sharding import PartitionSpec as P

RANK = 64
DOCS_DEV = 4
N_DP = 32
DOCS = N_DP * DOCS_DEV
Y = 4
TOKENS = 1024
STEP = 256
EARLY = 128
NT = (((1,), (1,)), ((), ()))


def swap(value, even, odd):
    return lax.ppermute(value, "tensor", [(i, i ^ (odd if i & 1 else even)) for i in range(8)])


def tokens(ref, start, count):
    return ref.at[pl.ds(pl.multiple_of(start, EARLY), count)]


def project_rows(grads, acts, wide_out, wide_in, start, count):
    here = pl.ds(start, count)
    return jnp.dot(grads[here], wide_out[...], preferred_element_type=jnp.float32) + jnp.dot(
        acts[here], wide_in[...], preferred_element_type=jnp.float32
    )


def project_early_kernel(
    out_grads, activations, proj_out, proj_in, send, first, grads_last, acts_last, wide_out, wide_in, grads, acts, raw_out, raw_in, sem
):
    half = TOKENS // 2
    core = lax.axis_index("tensor") & 1
    kept, sent = core * half, (1 - core) * half

    def copies(slot, start, count, to_grads, to_acts, place):
        return (
            pltpu.make_async_copy(tokens(out_grads, start, count), tokens(to_grads, place, count), sem.at[2 * slot]),
            pltpu.make_async_copy(tokens(activations, start, count), tokens(to_acts, place, count), sem.at[2 * slot + 1]),
        )

    def sent_copies(block):
        return copies(1 + block, sent + block * STEP, STEP, grads, acts, block * STEP)

    blocks = half // STEP
    weights = (
        pltpu.make_async_copy(proj_out, raw_out, sem.at[0]),
        pltpu.make_async_copy(proj_in, raw_in, sem.at[1]),
    )
    near = copies(1 + blocks, kept, EARLY, grads, acts, half)
    last = copies(2 + blocks, kept + EARLY, half - EARLY, grads_last, acts_last, 0)
    for copy in weights:
        copy.start()
    for block in range(blocks):
        for copy in sent_copies(block):
            copy.start()
    for copy in near + last:
        copy.start()
    for copy in weights:
        copy.wait()
    wide_out[...] = jnp.concatenate([raw_out[...], jnp.zeros_like(raw_out)], axis=0).T
    wide_in[...] = jnp.concatenate([jnp.zeros_like(raw_in), raw_in[...]], axis=0).T

    @pl.loop(0, blocks)
    def _(block):
        for copy in sent_copies(block):
            copy.wait()
        start = pl.multiple_of(block * STEP, STEP)
        send[pl.ds(start, STEP)] = project_rows(grads, acts, wide_out, wide_in, start, STEP)

    @pl.loop(0, 1)
    def _(_):
        for copy in near:
            copy.wait()
        first[...] = project_rows(grads, acts, wide_out, wide_in, half, EARLY)

    for copy in last:
        copy.wait()


def project_late_kernel(first, grads, acts, wide_out, wide_in, keep):
    keep[:EARLY] = first[...]
    keep[EARLY:] = project_rows(grads, acts, wide_out, wide_in, 0, grads.shape[0])


def project(out_grads, activations, proj_out, proj_in, meanwhile):
    d, ff = out_grads.shape[1], activations.shape[1]
    half = TOKENS // 2
    in_vmem, in_hbm = pl.BlockSpec(memory_space=pltpu.VMEM), pl.BlockSpec(memory_space=pltpu.HBM)
    args = [pltpu.with_memory_space_constraint(x, pltpu.HBM) for x in (out_grads, activations, proj_out, proj_in)]
    send, *rest = pl.pallas_call(
        project_early_kernel,
        in_specs=[in_hbm] * 4,
        out_specs=[in_vmem] * 6,
        out_shape=[
            pltpu.VMEM((half, 2 * RANK), jnp.float32),
            pltpu.VMEM((EARLY, 2 * RANK), jnp.float32),
            pltpu.VMEM((half - EARLY, d), jnp.bfloat16),
            pltpu.VMEM((half - EARLY, ff), jnp.bfloat16),
            pltpu.VMEM((d, 2 * RANK), jnp.bfloat16),
            pltpu.VMEM((ff, 2 * RANK), jnp.bfloat16),
        ],
        scratch_shapes=[
            pltpu.VMEM((half + EARLY, d), jnp.bfloat16),
            pltpu.VMEM((half + EARLY, ff), jnp.bfloat16),
            pltpu.VMEM((RANK, d), jnp.bfloat16),
            pltpu.VMEM((RANK, ff), jnp.bfloat16),
            pltpu.SemaphoreType.DMA((2 * (half // STEP + 3),)),
        ],
        compiler_params=pltpu.CompilerParams(vmem_limit_bytes=24 << 20),
        name="project_early",
    )(*args)
    got = meanwhile(send)
    keep = pl.pallas_call(
        project_late_kernel,
        in_specs=[in_vmem] * 5,
        out_specs=in_vmem,
        out_shape=pltpu.VMEM((half, 2 * RANK), jnp.float32),
        compiler_params=pltpu.CompilerParams(vmem_limit_bytes=24 << 20),
        cost_estimate=pl.CostEstimate(
            flops=2 * half * (d + ff) * 2 * RANK, bytes_accessed=2 * half * (d + ff), transcendentals=0
        ),
        name="project_late",
    )(*rest)
    return keep, got


def thirds(value):
    high = value.astype(jnp.bfloat16)
    rest = value - high.astype(jnp.float32)
    middle = rest.astype(jnp.bfloat16)
    return high, middle, (rest - middle.astype(jnp.float32)).astype(jnp.bfloat16)


def features_kernel(ids, total, more, feat):
    parts = thirds(total[...] + more[...])
    right = jnp.concatenate([part[:, RANK:] for part in parts], axis=1)

    def by_document(part):
        out_t = part.T[:RANK]
        return jnp.concatenate([jnp.where(ids[...] == d, out_t, jnp.zeros_like(out_t)) for d in range(DOCS_DEV)], axis=0)

    high, middle, low = [
        jnp.dot(by_document(part), right[:, : (3 - i) * RANK], preferred_element_type=jnp.float32)
        for i, part in enumerate(parts)
    ]
    least = (low + high[:, 2 * RANK :]) + middle[:, RANK:]
    feat[...] = least + ((middle[:, :RANK] + high[:, RANK : 2 * RANK]) + high[:, :RANK])


def features(ids, total, more):
    return pl.pallas_call(
        features_kernel,
        out_shape=jax.ShapeDtypeStruct((DOCS_DEV * RANK, RANK), jnp.float32),
        compiler_params=pltpu.CompilerParams(vmem_limit_bytes=16 << 20),
        name="features",
    )(ids, total, more)


def score_kernel(owners, feats, *refs):
    queries, (everyone, rows) = refs[:-2], refs[-2:]
    half, count = feats.shape[1], feats.shape[0] // 2
    each = queries[0].shape[0]
    here = lax.axis_index("dp") & (Y - 1)
    for step, q in enumerate(queries):
        for h in range(2):
            start = (h * Y + (here ^ step)) * each
            rows[pl.ds(pl.multiple_of(start, each), each)] = q[:, h * half : (h + 1) * half]
    every = lax.dot_general(feats[...], rows[...], NT, preferred_element_type=jnp.float32)
    width = rows.shape[0] // 2
    halves = jnp.concatenate([every[:, :width], every[:, width:]], axis=0)
    doc = lax.broadcasted_iota(jnp.int32, (count, 4 * count), 0)
    source = lax.broadcasted_iota(jnp.int32, (count, 4 * count), 1)
    first = (doc >> 2) * 8 + (doc & 3)
    spot = (source == first) | (source == first + 2 * count + 4)
    scored = jnp.dot(
        spot.astype(feats.dtype), jnp.concatenate(thirds(halves), axis=1), preferred_element_type=jnp.float32
    )
    scored = (scored[:, 2 * width :] + scored[:, width : 2 * width]) + scored[:, :width]
    scored = scored.astype(everyone.dtype).astype(jnp.float32)
    tiles = [scored[8 * x : 8 * x + 8] for x in range(count // 8)]
    lane = lax.broadcasted_iota(jnp.int32, tiles[0].shape, 1) >> 5
    packed = []
    for y in range(Y):
        total = jnp.zeros_like(tiles[0])
        for x, tile in enumerate(tiles):
            shift = (x - y) % Y * each
            total = jnp.where(lane == x, pltpu.roll(tile, shift, 1) if shift else tile, total)
        packed.append(total)
    for peer in range(N_DP):
        y = owners[:, peer : peer + 1] & (Y - 1)
        chosen = jnp.where(y < 2, jnp.where(y == 0, packed[0], packed[1]), jnp.where(y == 2, packed[2], packed[3]))
        everyone[peer] = chosen.astype(everyone.dtype)


def score(owners, feats, queries):
    rows = len(queries) * queries[0].shape[0]
    return pl.pallas_call(
        score_kernel,
        out_specs=pl.BlockSpec(memory_space=pltpu.VMEM),
        out_shape=pltpu.VMEM((N_DP, 8, 128), jnp.bfloat16),
        scratch_shapes=[pltpu.VMEM((2 * rows, feats.shape[1]), feats.dtype)],
        compiler_params=pltpu.CompilerParams(vmem_limit_bytes=16 << 20),
        name="score",
    )(owners, feats, *queries)


def place_kernel(owners, blocks, scores):
    rows = scores.shape[0]
    here = lax.broadcasted_iota(jnp.int32, owners.shape, 1) == lax.axis_index("dp")
    owner = jnp.sum(jnp.where(here, owners[...], 0), axis=1, keepdims=True)
    line = jnp.zeros((Y * 8, blocks.shape[2]), jnp.float32)
    for first in range(0, N_DP, Y):
        chosen = (owner & ~(Y - 1)) == first
        line = jnp.where(chosen, blocks[first : first + Y].astype(jnp.float32).reshape(line.shape), line)
    row = lax.broadcasted_iota(jnp.int32, (Y * 8, DOCS), 0)
    column = lax.broadcasted_iota(jnp.int32, (Y * 8, DOCS), 1)
    spot = (column & 31) == ((row >> 2) & 1) * 16 + (row >> 3) * 4 + (row & 3)
    wide = jnp.dot(line.T.astype(blocks.dtype), spot.astype(blocks.dtype), preferred_element_type=jnp.float32)
    group = lax.broadcasted_iota(jnp.int32, scores.shape, 1) >> 5
    total = wide[:rows]
    for x in range(1, DOCS // 32):
        total = jnp.where(group == x, wide[x * rows : (x + 1) * rows], total)
    scores[...] = total


def place(owners, blocks):
    return pl.pallas_call(
        place_kernel,
        out_shape=jax.ShapeDtypeStruct((32, DOCS), jnp.float32),
        compiler_params=pltpu.CompilerParams(vmem_limit_bytes=16 << 20),
        name="place",
    )(owners, blocks)


def spread_kernel(block, everyone):
    everyone[...] = jnp.broadcast_to(block[...], everyone.shape)


def spread(block, peers):
    return pl.pallas_call(
        spread_kernel,
        out_specs=pl.BlockSpec(memory_space=pltpu.VMEM),
        out_shape=pltpu.VMEM((peers,) + block.shape, block.dtype),
        compiler_params=pltpu.CompilerParams(vmem_limit_bytes=8 << 20),
        name="spread",
    )(block)


def shards(activations, out_grads, proj_in, proj_out, doc_ids, queries, block_owner):
    core0 = (lax.axis_index("tensor") & 1) == 0
    half = TOKENS // 2
    core0, proj_in = lax.optimization_barrier((core0, proj_in))

    keep, got = project(out_grads, activations, proj_out.T, proj_in.T, lambda send: swap(send, 1, 1))
    total = keep + got
    total = total + swap(total, 2, 6)
    more = swap(total, 6, 2)

    lines = [queries] + [lax.ppermute(queries, "dp", [(i, i ^ step) for i in range(N_DP)]) for step in range(1, Y)]

    ids = jnp.where(core0, doc_ids[:, :half], doc_ids[:, half:])
    more, lines = lax.optimization_barrier((more, lines))
    feat = features(ids, total, more)
    block = (feat + swap(feat, 1, 1)).astype(jnp.bfloat16)
    block = block.reshape(DOCS_DEV, 2, RANK * RANK // 2).transpose(1, 0, 2).reshape(2 * DOCS_DEV, RANK * RANK // 2)

    peers = N_DP // Y
    groups = [[g * Y + y for g in range(peers)] for y in range(Y)]
    feats = lax.all_to_all(spread(block, peers), "dp", 0, 0, axis_index_groups=groups)
    owners = block_owner.reshape(1, N_DP)
    blocks = score(owners, feats.reshape(peers * 2 * DOCS_DEV, RANK * RANK // 2), lines)

    return place(owners, lax.all_to_all(blocks, "dp", 0, 0))


def solution(mesh):
    placed = (
        P("dp", "tensor"),
        P("dp", "tensor"),
        P("tensor", None),
        P("tensor", None),
        P("dp", None),
        P(("dp", "tensor"), None),
        P(),
    )
    return jax.shard_map(
        shards, mesh=mesh, in_specs=placed, out_specs=P(("dp", "tensor"), None), check_vma=False
    )
```

```python
import jax
import jax.numpy as jnp
from jax import lax
from jax.experimental import pallas as pl
from jax.experimental.pallas import tpu as pltpu
from jax.sharding import PartitionSpec as P

RANK = 64
DOCS_DEV = 4
N_DP = 32
DOCS = N_DP * DOCS_DEV
Y = 4
TOKENS = 1024
STEP = 256
EARLY = 128
NT = (((1,), (1,)), ((), ()))


def swap(value, even, odd):
    return lax.ppermute(value, "tensor", [(i, i ^ (odd if i & 1 else even)) for i in range(8)])


def tokens(ref, start, count):
    return ref.at[pl.ds(pl.multiple_of(start, EARLY), count)]


def project_rows(grads, acts, wide_out, wide_in, start, count):
    here = pl.ds(start, count)
    return jnp.dot(grads[here], wide_out[...], preferred_element_type=jnp.float32) + jnp.dot(
        acts[here], wide_in[...], preferred_element_type=jnp.float32
    )


def project_early_kernel(
    out_grads, activations, proj_out, proj_in, send, first, grads_last, acts_last, wide_out, wide_in, grads, acts, raw_out, raw_in, sem
):
    half = TOKENS // 2
    core = lax.axis_index("tensor") & 1
    kept, sent = core * half, (1 - core) * half

    def copies(slot, start, count, to_grads, to_acts, place):
        return (
            pltpu.make_async_copy(tokens(out_grads, start, count), tokens(to_grads, place, count), sem.at[2 * slot]),
            pltpu.make_async_copy(tokens(activations, start, count), tokens(to_acts, place, count), sem.at[2 * slot + 1]),
        )

    def sent_copies(block):
        return copies(1 + block, sent + block * STEP, STEP, grads, acts, block * STEP)

    blocks = half // STEP
    weights = (
        pltpu.make_async_copy(proj_out, raw_out, sem.at[0]),
        pltpu.make_async_copy(proj_in, raw_in, sem.at[1]),
    )
    near = copies(1 + blocks, kept, EARLY, grads, acts, half)
    last = copies(2 + blocks, kept + EARLY, half - EARLY, grads_last, acts_last, 0)
    for copy in weights:
        copy.start()
    for block in range(blocks):
        for copy in sent_copies(block):
            copy.start()
    for copy in near + last:
        copy.start()
    for copy in weights:
        copy.wait()
    wide_out[...] = jnp.concatenate([raw_out[...], jnp.zeros_like(raw_out)], axis=0).T
    wide_in[...] = jnp.concatenate([jnp.zeros_like(raw_in), raw_in[...]], axis=0).T

    @pl.loop(0, blocks)
    def _(block):
        for copy in sent_copies(block):
            copy.wait()
        start = pl.multiple_of(block * STEP, STEP)
        send[pl.ds(start, STEP)] = project_rows(grads, acts, wide_out, wide_in, start, STEP)

    @pl.loop(0, 1)
    def _(_):
        for copy in near:
            copy.wait()
        first[...] = project_rows(grads, acts, wide_out, wide_in, half, EARLY)

    for copy in last:
        copy.wait()


def project_late_kernel(first, grads, acts, wide_out, wide_in, keep):
    keep[:EARLY] = first[...]
    keep[EARLY:] = project_rows(grads, acts, wide_out, wide_in, 0, grads.shape[0])


def project(out_grads, activations, proj_out, proj_in, meanwhile):
    d, ff = out_grads.shape[1], activations.shape[1]
    half = TOKENS // 2
    in_vmem, in_hbm = pl.BlockSpec(memory_space=pltpu.VMEM), pl.BlockSpec(memory_space=pltpu.HBM)
    args = [pltpu.with_memory_space_constraint(x, pltpu.HBM) for x in (out_grads, activations, proj_out, proj_in)]
    send, *rest = pl.pallas_call(
        project_early_kernel,
        in_specs=[in_hbm] * 4,
        out_specs=[in_vmem] * 6,
        out_shape=[
            pltpu.VMEM((half, 2 * RANK), jnp.float32),
            pltpu.VMEM((EARLY, 2 * RANK), jnp.float32),
            pltpu.VMEM((half - EARLY, d), jnp.bfloat16),
            pltpu.VMEM((half - EARLY, ff), jnp.bfloat16),
            pltpu.VMEM((d, 2 * RANK), jnp.bfloat16),
            pltpu.VMEM((ff, 2 * RANK), jnp.bfloat16),
        ],
        scratch_shapes=[
            pltpu.VMEM((half + EARLY, d), jnp.bfloat16),
            pltpu.VMEM((half + EARLY, ff), jnp.bfloat16),
            pltpu.VMEM((RANK, d), jnp.bfloat16),
            pltpu.VMEM((RANK, ff), jnp.bfloat16),
            pltpu.SemaphoreType.DMA((2 * (half // STEP + 3),)),
        ],
        compiler_params=pltpu.CompilerParams(vmem_limit_bytes=24 << 20),
        name="project_early",
    )(*args)
    got = meanwhile(send)
    keep = pl.pallas_call(
        project_late_kernel,
        in_specs=[in_vmem] * 5,
        out_specs=in_vmem,
        out_shape=pltpu.VMEM((half, 2 * RANK), jnp.float32),
        compiler_params=pltpu.CompilerParams(vmem_limit_bytes=24 << 20),
        cost_estimate=pl.CostEstimate(
            flops=2 * half * (d + ff) * 2 * RANK, bytes_accessed=2 * half * (d + ff), transcendentals=0
        ),
        name="project_late",
    )(*rest)
    return keep, got


def thirds(value):
    high = value.astype(jnp.bfloat16)
    rest = value - high.astype(jnp.float32)
    middle = rest.astype(jnp.bfloat16)
    return high, middle, (rest - middle.astype(jnp.float32)).astype(jnp.bfloat16)


def features_kernel(ids, total, more, feat, wide):
    parts = thirds(total[...] + more[...])
    right = jnp.concatenate([part[:, RANK:] for part in parts], axis=1)

    def by_document(part):
        out_t = part.T[:RANK]
        return jnp.concatenate([jnp.where(ids[...] == d, out_t, jnp.zeros_like(out_t)) for d in range(DOCS_DEV)], axis=0)

    high, middle, low = [
        jnp.dot(by_document(part), right[:, : (3 - i) * RANK], preferred_element_type=jnp.float32)
        for i, part in enumerate(parts)
    ]
    least = (low + high[:, 2 * RANK :]) + middle[:, RANK:]
    wide[...] = least + ((middle[:, :RANK] + high[:, RANK : 2 * RANK]) + high[:, :RANK])
    count = feat.shape[0]
    feat[...] = jnp.concatenate([wide[pl.ds(0, count, stride=2)], wide[pl.ds(1, count, stride=2)]], axis=1)


def features(ids, total, more):
    return pl.pallas_call(
        features_kernel,
        out_shape=jax.ShapeDtypeStruct((DOCS_DEV * RANK // 2, 2 * RANK), jnp.float32),
        scratch_shapes=[pltpu.VMEM((DOCS_DEV * RANK, RANK), jnp.float32)],
        compiler_params=pltpu.CompilerParams(vmem_limit_bytes=16 << 20),
        name="features",
    )(ids, total, more)


def score_kernel(owners, feats, *refs):
    queries, (everyone, rows) = refs[:-2], refs[-2:]
    half, count = feats.shape[1], feats.shape[0] // 2
    each = queries[0].shape[0]
    here = lax.axis_index("dp") & (Y - 1)
    for step, q in enumerate(queries):
        for h in range(2):
            start = (h * Y + (here ^ step)) * each
            rows[pl.ds(pl.multiple_of(start, each), each)] = q[:, h * half : (h + 1) * half]
    every = lax.dot_general(feats[...], rows[...], NT, preferred_element_type=jnp.float32)
    width = rows.shape[0] // 2
    halves = jnp.concatenate([every[:, :width], every[:, width:]], axis=0)
    doc = lax.broadcasted_iota(jnp.int32, (count, 4 * count), 0)
    source = lax.broadcasted_iota(jnp.int32, (count, 4 * count), 1)
    first = (doc >> 2) * 8 + (doc & 3)
    spot = (source == first) | (source == first + 2 * count + 4)
    scored = jnp.dot(
        spot.astype(feats.dtype), jnp.concatenate(thirds(halves), axis=1), preferred_element_type=jnp.float32
    )
    scored = (scored[:, 2 * width :] + scored[:, width : 2 * width]) + scored[:, :width]
    scored = scored.astype(everyone.dtype).astype(jnp.float32)
    tiles = [scored[8 * x : 8 * x + 8] for x in range(count // 8)]
    lane = lax.broadcasted_iota(jnp.int32, tiles[0].shape, 1) >> 5
    packed = []
    for y in range(Y):
        total = jnp.zeros_like(tiles[0])
        for x, tile in enumerate(tiles):
            shift = (x - y) % Y * each
            total = jnp.where(lane == x, pltpu.roll(tile, shift, 1) if shift else tile, total)
        packed.append(total)
    for peer in range(N_DP):
        y = owners[:, peer : peer + 1] & (Y - 1)
        chosen = jnp.where(y < 2, jnp.where(y == 0, packed[0], packed[1]), jnp.where(y == 2, packed[2], packed[3]))
        everyone[peer] = chosen.astype(everyone.dtype)


def score(owners, feats, queries):
    rows = len(queries) * queries[0].shape[0]
    return pl.pallas_call(
        score_kernel,
        out_specs=pl.BlockSpec(memory_space=pltpu.VMEM),
        out_shape=pltpu.VMEM((N_DP, 8, 128), jnp.bfloat16),
        scratch_shapes=[pltpu.VMEM((2 * rows, feats.shape[1]), feats.dtype)],
        compiler_params=pltpu.CompilerParams(vmem_limit_bytes=16 << 20),
        name="score",
    )(owners, feats, *queries)


def place_kernel(owners, blocks, scores):
    rows = scores.shape[0]
    here = lax.broadcasted_iota(jnp.int32, owners.shape, 1) == lax.axis_index("dp")
    owner = jnp.sum(jnp.where(here, owners[...], 0), axis=1, keepdims=True)
    line = jnp.zeros((Y * 8, blocks.shape[2]), jnp.float32)
    for first in range(0, N_DP, Y):
        chosen = (owner & ~(Y - 1)) == first
        line = jnp.where(chosen, blocks[first : first + Y].astype(jnp.float32).reshape(line.shape), line)
    row = lax.broadcasted_iota(jnp.int32, (Y * 8, DOCS), 0)
    column = lax.broadcasted_iota(jnp.int32, (Y * 8, DOCS), 1)
    spot = (column & 31) == ((row >> 2) & 1) * 16 + (row >> 3) * 4 + (row & 3)
    wide = jnp.dot(line.T.astype(blocks.dtype), spot.astype(blocks.dtype), preferred_element_type=jnp.float32)
    group = lax.broadcasted_iota(jnp.int32, scores.shape, 1) >> 5
    total = wide[:rows]
    for x in range(1, DOCS // 32):
        total = jnp.where(group == x, wide[x * rows : (x + 1) * rows], total)
    scores[...] = total


def place(owners, blocks):
    return pl.pallas_call(
        place_kernel,
        out_shape=jax.ShapeDtypeStruct((32, DOCS), jnp.float32),
        compiler_params=pltpu.CompilerParams(vmem_limit_bytes=16 << 20),
        name="place",
    )(owners, blocks)


def spread_kernel(block, everyone):
    everyone[...] = jnp.broadcast_to(block[...], everyone.shape)


def spread(block, peers):
    return pl.pallas_call(
        spread_kernel,
        out_specs=pl.BlockSpec(memory_space=pltpu.VMEM),
        out_shape=pltpu.VMEM((peers,) + block.shape, block.dtype),
        compiler_params=pltpu.CompilerParams(vmem_limit_bytes=8 << 20),
        name="spread",
    )(block)


def shards(activations, out_grads, proj_in, proj_out, doc_ids, queries, block_owner):
    core0 = (lax.axis_index("tensor") & 1) == 0
    half = TOKENS // 2
    core0, proj_in = lax.optimization_barrier((core0, proj_in))

    keep, got = project(out_grads, activations, proj_out.T, proj_in.T, lambda send: swap(send, 1, 1))
    total = keep + got
    total = total + swap(total, 2, 6)
    more = swap(total, 6, 2)

    lines = [queries] + [lax.ppermute(queries, "dp", [(i, i ^ step) for i in range(N_DP)]) for step in range(1, Y)]

    ids = jnp.where(core0, doc_ids[:, :half], doc_ids[:, half:])
    more, lines = lax.optimization_barrier((more, lines))
    feat = features(ids, total, more)
    block = (feat + swap(feat, 1, 1)).astype(jnp.bfloat16)
    block = block.reshape(DOCS_DEV, 2, RANK * RANK // 2).transpose(1, 0, 2).reshape(2 * DOCS_DEV, RANK * RANK // 2)

    peers = N_DP // Y
    groups = [[g * Y + y for g in range(peers)] for y in range(Y)]
    feats = lax.all_to_all(spread(block, peers), "dp", 0, 0, axis_index_groups=groups)
    owners = block_owner.reshape(1, N_DP)
    blocks = score(owners, feats.reshape(peers * 2 * DOCS_DEV, RANK * RANK // 2), lines)

    return place(owners, lax.all_to_all(blocks, "dp", 0, 0))


def solution(mesh):
    placed = (
        P("dp", "tensor"),
        P("dp", "tensor"),
        P("tensor", None),
        P("tensor", None),
        P("dp", None),
        P(("dp", "tensor"), None),
        P(),
    )
    return jax.shard_map(
        shards, mesh=mesh, in_specs=placed, out_specs=P(("dp", "tensor"), None), check_vma=False
    )
```
